128 devices in a mesh: segment: 4 (over z), space: 32 (over y, x, core).
Axes of the slice: x: 4, y: 4, z: 4, core: 2. Of those that a mesh axis runs over, the one named last changes fastest.
Arguments:
- text_states: bfloat16 [2, 32, 128, 4096], P(None, 'space'), may hold values from -6 to 6
- token_ids: int32 [2, 32, 128], replicated, may hold values from 0 to 32127, as said below
- step_ids: int32 [3, 2], replicated, may hold values from 100 to 899
- base_noise: bfloat16 [2, 32, 3, 1024], P(None, 'space'), may hold values from -6 to 6
- upscale_noise: bfloat16 [2, 32, 3, 1024], P(None, 'space'), may hold values from -6 to 6
- final_noise: bfloat16 [2, 32, 3, 512, 32], P(None, None, None, 'space'), may hold values from -6 to 6
- t5_gain: float32 [4096], replicated, may hold values from 0.5 to 1.5
- base_keyval: bfloat16 [4096, 1024], replicated, may hold values from -0.09375 to 0.09375
- upscale_keyval: bfloat16 [2, 4096, 256], replicated, may hold values from -0.09375 to 0.09375
- base_input: bfloat16 [3, 512], replicated, may hold values from -3.5 to 3.5
- base_time: bfloat16 [512, 512], replicated, may hold values from -0.25 to 0.25
- base_gain: float32 [3, 512], replicated, may hold values from 0.5 to 1.5
- base_conv: bfloat16 [9, 512, 512], replicated, may hold values from -0.09375 to 0.09375
- base_query: bfloat16 [512, 512], replicated, may hold values from -0.25 to 0.25
- base_output: bfloat16 [512, 512], replicated, may hold values from -0.25 to 0.25
- base_head: bfloat16 [512, 3], replicated, may hold values from -0.25 to 0.25
- upscale_input: bfloat16 [2, 6, 128], replicated, may hold values from -2.5 to 2.5
- upscale_time: bfloat16 [2, 128, 128], replicated, may hold values from -0.5 to 0.5
- upscale_gain: float32 [2, 3, 128], replicated, may hold values from 0.5 to 1.5
- upscale_conv: bfloat16 [2, 9, 128, 128], replicated, may hold values from -0.1875 to 0.1875
- upscale_query: bfloat16 [2, 128, 128], replicated, may hold values from -0.5 to 0.5
- upscale_output: bfloat16 [2, 128, 128], replicated, may hold values from -0.5 to 0.5
- upscale_head: bfloat16 [2, 128, 3], replicated, may hold values from -0.5 to 0.5
Outputs:
- early_states: bfloat16 [2, 2, 32, 3, 1024], P(None, None, 'space', None, 'segment')
- final_states: bfloat16 [2, 2, 32, 3, 512, 32], P(None, None, 'segment', None, 'space')
The draws below stay inside these ranges and needn't reach their ends.
Inputs may be any that keep to these rules, and one draw needn't show every extreme that they name: `token_ids`: each prompt's ids are nonzero on its first 1 to 128 positions and 0 (padding) after them; some prompt fills all 128 positions.
All inputs are finite; a program needn't handle non-finite values.
Results may differ from the reference program's by a relative error of at most 0.0095.
Values may be sent and summed in bfloat16 or wider, within the bound.
A program may use at most 256 MiB of HBM per device.

```python
import math
import jax
import jax.numpy as jnp
from jax import lax

DT5 = 4096
VOCAB = 32128
CB = 512
CS = 128
HD = 64
LTXT = 128
SIDE = 32
ROWS2 = 512
WIN2 = 32
MICRO = 2
PX = 1024
IMGS = 32


def draw_token_ids(key, part):
    length_key = jax.random.fold_in(key, 11)
    word_key = jax.random.fold_in(key, 12)
    lengths = jax.random.randint(length_key, (MICRO, IMGS), 1, LTXT + 1)
    lengths = lengths.at[0, 0].set(LTXT)
    words = jax.random.randint(word_key, (MICRO, IMGS, LTXT), 1, VOCAB)
    position = jnp.arange(LTXT, dtype=jnp.int32)
    return jnp.where(position[None, None, :] < lengths[:, :, None], words, 0).astype(jnp.int32)


def place_ends(array, key, least, top_value):
    extent = array.shape
    index_at = [jax.random.randint(jax.random.fold_in(key, axis), (), 0, extent[axis]) for axis in range(len(extent))]
    array = array.at[tuple(index_at)].set(least)
    longest = extent.index(max(extent))
    index_at[longest] = (index_at[longest] + 1) % extent[longest]
    return array.at[tuple(index_at)].set(top_value)


def levels(key, shape, pieces, smallest, largest):
    def one(axis_at, parts):
        draws = jax.random.uniform(jax.random.fold_in(jax.random.fold_in(key, 6), axis_at), (parts,), jnp.float32, smallest / len(pieces), largest / len(pieces))
        return jnp.repeat(jnp.exp(draws), shape[axis_at] // parts).reshape((-1,) + (1,) * (len(shape) - axis_at - 1))

    level = one(*pieces[0])
    for cut in pieces[1:]:
        level = level * one(*cut)
    return level


def bell_draw(key, dims, scale, limit, shards=(), held_as=jnp.bfloat16):
    array = scale * jax.random.normal(key, dims, jnp.float32)
    if shards:
        array = array * levels(key, dims, shards, -0.22, 0.18)
    return jnp.clip(array, -limit, limit).astype(held_as)


def setup_inputs(seed: int = 0) -> dict:
    seeds = jax.random.split(jax.random.key(seed), 24)
    return {
        "text_states": bell_draw(seeds[0], (MICRO, IMGS, LTXT, DT5), 1.0, 6.0, ((1, 32),)),
        "token_ids": draw_token_ids(jax.random.fold_in(seeds[23], 71), 0),
        "step_ids": place_ends(jax.random.randint(seeds[2], (3, MICRO), 100, 900), jax.random.fold_in(seeds[2], 1), 100, 899).astype(jnp.int32),
        "base_noise": bell_draw(seeds[3], (MICRO, IMGS, 3, PX), 1.0, 6.0, ((1, 32),)),
        "upscale_noise": bell_draw(seeds[4], (MICRO, IMGS, 3, PX), 1.0, 6.0, ((1, 32),)),
        "final_noise": bell_draw(seeds[5], (MICRO, IMGS, 3, ROWS2, WIN2), 1.0, 6.0, ((3, 32),)),
        "t5_gain": jnp.clip(1.0 + 0.1 * jax.random.normal(seeds[6], (DT5,), jnp.float32), 0.5, 1.5),
        "base_keyval": bell_draw(seeds[7], (DT5, 2 * CB), DT5 ** -0.5, 0.09375),
        "upscale_keyval": bell_draw(seeds[8], (2, DT5, 2 * CS), DT5 ** -0.5, 0.09375),
        "base_input": bell_draw(seeds[9], (3, CB), 3 ** -0.5, 3.5),
        "base_time": bell_draw(seeds[10], (CB, CB), CB ** -0.5, 0.25),
        "base_gain": jnp.clip(1.0 + 0.1 * jax.random.normal(seeds[11], (3, CB), jnp.float32), 0.5, 1.5),
        "base_conv": bell_draw(seeds[12], (9, CB, CB), (9 * CB) ** -0.5, 0.09375),
        "base_query": bell_draw(seeds[13], (CB, CB), CB ** -0.5, 0.25),
        "base_output": bell_draw(seeds[14], (CB, CB), CB ** -0.5, 0.25),
        "base_head": bell_draw(seeds[15], (CB, 3), CB ** -0.5, 0.25),
        "upscale_input": bell_draw(seeds[16], (2, 6, CS), 6 ** -0.5, 2.5),
        "upscale_time": bell_draw(seeds[17], (2, CS, CS), CS ** -0.5, 0.5),
        "upscale_gain": jnp.clip(1.0 + 0.1 * jax.random.normal(seeds[18], (2, 3, CS), jnp.float32), 0.5, 1.5),
        "upscale_conv": bell_draw(seeds[19], (2, 9, CS, CS), (9 * CS) ** -0.5, 0.1875),
        "upscale_query": bell_draw(seeds[20], (2, CS, CS), CS ** -0.5, 0.5),
        "upscale_output": bell_draw(seeds[21], (2, CS, CS), CS ** -0.5, 0.5),
        "upscale_head": bell_draw(seeds[22], (2, CS, 3), CS ** -0.5, 0.5),
    }


def rms_scale(hidden, gain):
    return hidden * lax.rsqrt(lax.optimization_barrier(jnp.mean(hidden * hidden, axis=-1, keepdims=True)) + 1e-06) * gain

def alpha_bar(step):
    frac = (step.astype(jnp.float32) / 1000.0 + 0.008) / 1.008
    return jnp.cos(frac * (math.pi / 2)) ** 2

def time_embed(step, w_time):
    half = w_time.shape[0] // 2
    freqs = jnp.exp(-math.log(10000.0) * jnp.arange(half, dtype=jnp.float32) / half)
    angle = step.astype(jnp.float32) * freqs
    embed = jnp.concatenate([jnp.sin(angle), jnp.cos(angle)])[None, :].astype(jnp.bfloat16)
    return jnp.dot(embed, w_time, preferred_element_type=jnp.float32)

def pixel_rows(planes):
    return planes.reshape(planes.shape[0], -1).T

def upsample(region, height, width, rise, spread):
    grid = region.reshape(3, height, width)
    return jnp.repeat(jnp.repeat(grid, rise, axis=1), spread, axis=2)

def conv_padded(padded, w_conv):
    count = padded.shape[0]
    height = padded.shape[1] - 2
    width = padded.shape[2] - 2
    chans = padded.shape[3]
    taps = [padded[:, tap // 3:tap // 3 + height, tap % 3:tap % 3 + width, :] for tap in range(9)]
    stacked = jnp.concatenate(taps, axis=-1).reshape(count * height * width, 9 * chans)
    return jnp.dot(stacked, w_conv.reshape(9 * chans, -1), preferred_element_type=jnp.float32)

def attend(query, keyval, valid):
    count, rows, width = query.shape
    heads = width // HD
    q_four = query.astype(jnp.float32).reshape(count, rows, heads, HD)
    k_four = keyval[:, :, :width].astype(jnp.float32).reshape(count, -1, heads, HD)
    v_four = keyval[:, :, width:].astype(jnp.float32).reshape(count, -1, heads, HD)
    scores = jnp.einsum('bphd,blhd->bhpl', q_four, k_four)
    scores = jnp.where(valid[:, None, None, :], scores, -1e+30)
    weights = jax.nn.softmax(scores, axis=-1).astype(jnp.bfloat16)
    mixed = jnp.einsum('bhpl,blhd->bphd', weights.astype(jnp.float32), v_four)
    return mixed.reshape(count, rows, width).astype(jnp.bfloat16)

def front(pixels_in, step, weights):
    hidden = jnp.dot(pixels_in, weights[0], preferred_element_type=jnp.float32) + time_embed(step, weights[1])
    active = jax.nn.silu(rms_scale(hidden, weights[2][0])).astype(jnp.bfloat16)
    return (hidden, active)

def back(hidden, conv_sum, keyval, valid, noisy, step, weights):
    gains = weights[2]
    width = weights[4].shape[0]
    hidden = hidden + conv_sum
    query = jnp.dot(rms_scale(hidden, gains[1]).astype(jnp.bfloat16), weights[4], preferred_element_type=jnp.float32)
    query = (query * HD ** (-0.5)).astype(jnp.bfloat16)
    mixed = attend(query.reshape(keyval.shape[0], -1, width), keyval, valid)
    hidden = hidden + jnp.dot(mixed.reshape(-1, width), weights[5], preferred_element_type=jnp.float32)
    predicted = jnp.dot(rms_scale(hidden, gains[2]).astype(jnp.bfloat16), weights[6], preferred_element_type=jnp.float32)
    level = alpha_bar(step)
    earlier = alpha_bar(step - 50)
    clean = jnp.clip((noisy.astype(jnp.float32) - jnp.sqrt(1.0 - level) * predicted) / jnp.sqrt(level), -1.0, 1.0)
    prior = jnp.sqrt(earlier) * clean + jnp.sqrt(1.0 - earlier) * predicted
    return (clean.astype(jnp.bfloat16).T, prior.astype(jnp.bfloat16).T)

def local_section(noisy_planes, cond_planes, keyval, valid, step, weights):
    height, width = (noisy_planes.shape[1], noisy_planes.shape[2])
    planes = noisy_planes if cond_planes is None else jnp.concatenate([noisy_planes, cond_planes], axis=0)
    hidden, active = front(pixel_rows(planes), step, weights)
    padded = jnp.pad(active.reshape(1, height, width, -1), ((0, 0), (1, 1), (1, 1), (0, 0)))
    conv_sum = conv_padded(padded, weights[3])
    return back(hidden, conv_sum, keyval[None], valid[None], pixel_rows(noisy_planes), step, weights)

def project(context, weight):
    return jnp.dot(context, weight, preferred_element_type=jnp.float32).astype(jnp.bfloat16)

def reference(text_states, token_ids, step_ids, base_noise, upscale_noise, final_noise, t5_gain, base_keyval, upscale_keyval, base_input, base_time, base_gain, base_conv, base_query, base_output, base_head, upscale_input, upscale_time, upscale_gain, upscale_conv, upscale_query, upscale_output, upscale_head):
    quarter = SIDE // 4
    base_weights = (base_input, base_time, base_gain, base_conv, base_query, base_output, base_head)
    stacked = (upscale_input, upscale_time, upscale_gain, upscale_conv, upscale_query, upscale_output, upscale_head)
    first_weights = tuple((weight[0] for weight in stacked))
    last_weights = tuple((weight[1] for weight in stacked))

    def one_image(flat):
        micro = flat // IMGS
        image = flat % IMGS
        valid = token_ids[micro, image] != 0
        context = rms_scale(text_states[micro, image].astype(jnp.float32), t5_gain).astype(jnp.bfloat16)
        key_base = project(context, base_keyval)
        key_first = project(context, upscale_keyval[0])
        key_last = project(context, upscale_keyval[1])
        clean_base, prior_base = local_section(base_noise[micro, image].reshape(3, SIDE, SIDE), None, key_base, valid, step_ids[0, micro], base_weights)
        cond_first = upsample(clean_base.reshape(3, SIDE, SIDE)[:, :quarter, :quarter], quarter, quarter, 4, 4)
        clean_first, prior_first = local_section(upscale_noise[micro, image].reshape(3, SIDE, SIDE), cond_first, key_first, valid, step_ids[1, micro], first_weights)
        cond_last = upsample(clean_first, SIDE, SIDE, ROWS2 // SIDE, WIN2 // SIDE)
        clean_last, prior_last = local_section(final_noise[micro, image], cond_last, key_last, valid, step_ids[2, micro], last_weights)
        return (prior_base, prior_first, clean_last, prior_last)
    prior_base, prior_first, clean_last, prior_last = lax.map(one_image, jnp.arange(MICRO * IMGS, dtype=jnp.int32))
    early_states = jnp.stack([prior_base, prior_first]).reshape(2, MICRO, IMGS, 3, PX)
    final_states = jnp.stack([clean_last, prior_last]).reshape(2, MICRO, IMGS, 3, ROWS2, WIN2)
    return (early_states, final_states)
```

```python
import math

import jax
import jax.numpy as jnp
from jax import lax
from jax.sharding import PartitionSpec as P

HD = 64
SIDE = 32


def rms_scale(hidden, gain):
    return hidden * lax.rsqrt(jnp.mean(hidden * hidden, axis=-1, keepdims=True) + 1e-06) * gain


def alpha_bar(step):
    frac = (step.astype(jnp.float32) / 1000.0 + 0.008) / 1.008
    return jnp.cos(frac * (math.pi / 2)) ** 2


def time_embed(step, w_time):
    half = w_time.shape[0] // 2
    freqs = jnp.exp(-math.log(10000.0) * jnp.arange(half, dtype=jnp.float32) / half)
    angle = step.astype(jnp.float32)[:, None] * freqs
    embed = jnp.concatenate([jnp.sin(angle), jnp.cos(angle)], axis=1).astype(jnp.bfloat16)
    return jnp.dot(embed, w_time, preferred_element_type=jnp.float32)


def front(planes, steps, weights, inside):
    pixels = planes.transpose(0, 2, 3, 1)
    hidden = jnp.dot(pixels, weights[0], preferred_element_type=jnp.float32)
    hidden = hidden + time_embed(steps, weights[1])[:, None, None, :]
    active = jax.nn.silu(rms_scale(hidden, weights[2][0])).astype(jnp.bfloat16)
    active = jnp.where(inside[None, :, :, None], active, 0)
    return hidden, active


def conv(active, w_conv, height, width):
    chans = active.shape[-1]
    taps = [active[:, t // 3 : t // 3 + height, t % 3 : t % 3 + width, :] for t in range(9)]
    stacked = jnp.concatenate(taps, axis=-1)
    return jnp.dot(stacked, w_conv.reshape(9 * chans, -1), preferred_element_type=jnp.float32)


def attend(query, keyval, valid):
    count, rows, width = query.shape
    heads = width // HD
    q_four = query.reshape(count, rows, heads, HD)
    k_four = keyval[:, :, :width].reshape(count, -1, heads, HD)
    v_four = keyval[:, :, width:].reshape(count, -1, heads, HD)
    scores = jnp.einsum("bphd,blhd->bhpl", q_four, k_four, preferred_element_type=jnp.float32)
    scores = jnp.where(valid[:, None, None, :], scores, -1e30)
    weights = jax.nn.softmax(scores, axis=-1).astype(jnp.bfloat16)
    mixed = jnp.einsum("bhpl,blhd->bphd", weights, v_four, preferred_element_type=jnp.float32)
    return mixed.reshape(count, rows, width).astype(jnp.bfloat16)


def back(hidden, conv_sum, keyval, valid, noisy, steps, weights):
    gains = weights[2]
    micro, height, width, chans = hidden.shape
    hidden = (hidden + conv_sum).reshape(micro, -1, chans)
    query = jnp.dot(
        rms_scale(hidden, gains[1]).astype(jnp.bfloat16), weights[4], preferred_element_type=jnp.float32
    )
    query = (query * HD ** (-0.5)).astype(jnp.bfloat16)
    mixed = attend(query, keyval, valid)
    hidden = hidden + jnp.dot(mixed, weights[5], preferred_element_type=jnp.float32)
    predicted = jnp.dot(
        rms_scale(hidden, gains[2]).astype(jnp.bfloat16), weights[6], preferred_element_type=jnp.float32
    )
    predicted = predicted.transpose(0, 2, 1).reshape(micro, 3, height, width)
    level = alpha_bar(steps)[:, None, None, None]
    earlier = alpha_bar(steps - 50)[:, None, None, None]
    clean = jnp.clip(
        (noisy.astype(jnp.float32) - jnp.sqrt(1.0 - level) * predicted) / jnp.sqrt(level), -1.0, 1.0
    )
    prior = jnp.sqrt(earlier) * clean + jnp.sqrt(1.0 - earlier) * predicted
    return clean.astype(jnp.bfloat16), prior.astype(jnp.bfloat16)


def row_window(planes, start, count, axis):
    pad = [(0, 0)] * planes.ndim
    pad[axis] = (2, 2)
    return lax.dynamic_slice_in_dim(jnp.pad(planes, pad), start + 2, count, axis)


def shards(
    text_states, token_ids, step_ids, base_noise, upscale_noise, final_noise, t5_gain,
    base_keyval, upscale_keyval, base_input, base_time, base_gain, base_conv, base_query,
    base_output, base_head, upscale_input, upscale_time, upscale_gain, upscale_conv,
    upscale_query, upscale_output, upscale_head,
):
    groups = lax.axis_size("space")
    seg = lax.axis_size("segment")
    z = lax.axis_index("segment")
    place = lax.axis_index("space")
    micro = base_noise.shape[0]
    rows_dev = final_noise.shape[3]
    cols = final_noise.shape[4]
    lane = groups // seg
    own = SIDE // seg
    tall = rows_dev * lane
    base_weights = (base_input, base_time, base_gain, base_conv, base_query, base_output, base_head)
    stacked = (upscale_input, upscale_time, upscale_gain, upscale_conv, upscale_query, upscale_output, upscale_head)
    first_weights = tuple(w[0] for w in stacked)
    last_weights = tuple(w[1] for w in stacked)
    valid = lax.dynamic_index_in_dim(token_ids, place, 1, keepdims=False) != 0

    circles = [[y * lane + i for i in range(lane)] for y in range(seg)]
    swap = [(a * groups + b * lane + i, b * groups + a * lane + i) for a in range(seg) for b in range(seg) for i in range(lane)]
    both = ("segment", "space")
    up = [(i, i + 1) for i in range(seg - 1)]
    down = [(i + 1, i) for i in range(seg - 1)]

    mine = lax.dynamic_slice_in_dim(final_noise, z * lane, lane, 1)
    got = lax.all_to_all(mine, "space", split_axis=1, concat_axis=1, axis_index_groups=circles, tiled=True)
    got = lax.ppermute(got, both, swap)
    noise = got.transpose(0, 2, 1, 3, 4).reshape(micro, 3, tall, cols)
    above = lax.ppermute(noise[:, :, -1:], "segment", up)
    below = lax.ppermute(noise[:, :, :1], "segment", down)
    noise_ext = jnp.concatenate([above, noise, below], axis=2)

    states = text_states[:, 0]
    context = rms_scale(states.astype(jnp.float32), t5_gain).astype(jnp.bfloat16)

    def project(w):
        return jnp.dot(context, w, preferred_element_type=jnp.float32).astype(jnp.bfloat16)

    key_base, key_first, key_last = project(base_keyval), project(upscale_keyval[0]), project(upscale_keyval[1])

    grid = base_noise[:, 0].reshape(micro, 3, SIDE, SIDE)
    start = z * own

    def base_on(rows_first, height, width):
        window = row_window(grid, rows_first - 1, height + 2, 2)
        window = jnp.pad(window, ((0, 0), (0, 0), (0, 0), (1, 1)))[..., : width + 2]
        line = rows_first - 1 + jnp.arange(height + 2)
        col = jnp.arange(width + 2)
        inside = ((line >= 0) & (line < SIDE))[:, None] & ((col >= 1) & (col <= SIDE))[None]
        hidden, active = front(window, step_ids[0], base_weights, inside)
        total = conv(active, base_conv, height, width)
        hidden = hidden[:, 1 : 1 + height, 1 : 1 + width]
        return back(hidden, total, key_base, valid, window[:, :, 1 : 1 + height, 1 : 1 + width], step_ids[0], base_weights)

    _, base_prior = base_on(start, own, SIDE)
    region, _ = base_on(jnp.int32(0), SIDE // 4, SIDE // 4)

    cond = jnp.repeat(jnp.repeat(region, 4, axis=2), 4, axis=3)
    planes = jnp.concatenate([upscale_noise[:, 0].reshape(micro, 3, SIDE, SIDE), cond], axis=1)
    height = own + 2
    window = row_window(planes, start - 2, height + 2, 2)
    window = jnp.pad(window, ((0, 0), (0, 0), (0, 0), (1, 1)))
    line = start - 2 + jnp.arange(height + 2)
    col = jnp.arange(SIDE + 2)
    inside = ((line >= 0) & (line < SIDE))[:, None] & ((col >= 1) & (col <= SIDE))[None]
    hidden, active = front(window, step_ids[1], first_weights, inside)
    total = conv(active, first_weights[3], height, SIDE)
    clean_first, first_prior = back(
        hidden[:, 1:-1, 1:-1], total, key_first, valid, window[:, :3, 1:-1, 1:-1], step_ids[1], first_weights
    )
    first_prior = first_prior[:, :, 1 : 1 + own]

    cond = jnp.repeat(clean_first, tall // own, axis=2)[:, :, tall // own - 1 : tall // own + tall + 1]
    planes = jnp.pad(jnp.concatenate([noise_ext, cond], axis=1), ((0, 0), (0, 0), (0, 0), (1, 1)))
    line = z * tall - 1 + jnp.arange(tall + 2)
    col = jnp.arange(cols + 2)
    inside = ((line >= 0) & (line < tall * seg))[:, None] & ((col >= 1) & (col <= cols))[None]
    hidden, active = front(planes, step_ids[2], last_weights, inside)
    total = conv(active, last_weights[3], tall, cols)
    clean, prior = back(hidden[:, 1:-1, 1:-1], total, key_last, valid, noise, step_ids[2], last_weights)

    out = jnp.stack([clean, prior])
    out = lax.ppermute(out, both, swap)
    out = out.reshape(2, micro, 3, lane, rows_dev, cols).transpose(0, 1, 3, 2, 4, 5)
    final_states = lax.all_to_all(out, "space", split_axis=2, concat_axis=2, axis_index_groups=circles, tiled=True)
    early = jnp.stack([base_prior, first_prior]).reshape(2, micro, 1, 3, own * SIDE)
    return early, final_states


def solution(mesh):
    placed = [P() for _ in range(23)]
    placed[0] = placed[3] = placed[4] = P(None, "space", None, None)
    placed[5] = P(None, None, None, "space", None)
    return jax.shard_map(
        shards,
        mesh=mesh,
        in_specs=tuple(placed),
        out_specs=(
            P(None, None, "space", None, "segment"),
            P(None, None, "segment", None, "space", None),
        ),
        check_vma=False,
    )
```

```python
import functools
import math

import jax
import jax.numpy as jnp
from jax import lax
from jax.experimental import pallas as pl
from jax.experimental.pallas import tpu as pltpu
from jax.sharding import PartitionSpec as P

MESH = pl.DeviceIdType.MESH
ANY = pl.BlockSpec(memory_space=pl.ANY)
VMEM = pl.BlockSpec(memory_space=pltpu.VMEM)
SMEM = pl.BlockSpec(memory_space=pltpu.SMEM)
F32, BF16 = jnp.float32, jnp.bfloat16
LOG2E = 1.4426950408889634
SCALE = 0.125 * LOG2E
SEG, LANE = 4, 8
STEPS = 4


def dot(a, b):
    return jnp.dot(a, b, preferred_element_type=F32)


def dot_nt(a, b):
    return lax.dot_general(a, b, (((1,), (1,)), ((), ())), preferred_element_type=F32)


def iota(shape, dim):
    return lax.broadcasted_iota(jnp.int32, shape, dim)


def place():
    z = lax.axis_index("segment")
    p = lax.axis_index("space")
    return z, p // LANE, p % LANE


def remote(src, dst, send, recv, z, p):
    return pltpu.make_async_remote_copy(
        src_ref=src, dst_ref=dst, send_sem=send, recv_sem=recv, device_id=(z, p), device_id_type=MESH
    )


def gather_kernel(noise, got, send, recv, halo_send, own_sem):
    z, y, k = place()
    barrier = pltpu.get_barrier_semaphore()
    for j in range(LANE):
        @pl.when((y != z) | (k != j))
        def _():
            pl.semaphore_signal(barrier, inc=1, device_id=(y, z * LANE + j), device_id_type=MESH)

    @pl.when(z > 0)
    def _():
        pl.semaphore_signal(barrier, inc=1, device_id=(y, z * LANE - 1), device_id_type=MESH)

    @pl.when(z < SEG - 1)
    def _():
        pl.semaphore_signal(barrier, inc=1, device_id=(y, z * LANE + LANE), device_id_type=MESH)

    lower = (k == LANE - 1) & (y < SEG - 1)
    upper = (k == 0) & (y > 0)
    extra = jnp.where(lower | upper, LANE, 0)
    pl.semaphore_wait(barrier, LANE - 1 + jnp.where(y != z, 1, 0) + extra)

    def main(j):
        return remote(noise.at[:, z * LANE + j], got.at[k], send.at[j], recv.at[k], y, z * LANE + j)

    def halo(j, slot, to):
        return remote(noise.at[:, z * LANE + j], got.at[slot], halo_send.at[j], recv.at[slot], to, z * LANE + j)

    own = pltpu.make_async_copy(noise.at[:, z * LANE + k], got.at[k], own_sem)
    for j in range(LANE):
        @pl.when((y != z) | (k != j))
        def _():
            main(j).start()

    @pl.when(y == z)
    def _():
        own.start()

    for cond, slot, step in ((lower, LANE, 1), (upper, LANE + 1, -1)):
        @pl.when(cond)
        def _():
            for j in range(LANE):
                halo(j, slot, y + step).start()

    for j in range(LANE):
        @pl.when((y != z) | (k != j))
        def _():
            main(j).wait_send()
            remote(noise.at[:, z * LANE + j], got.at[j], send.at[j], recv.at[j], y, z * LANE + j).wait_recv()

    @pl.when(y == z)
    def _():
        own.wait()

    for cond, slot, step in ((lower, LANE, 1), (upper, LANE + 1, -1)):
        @pl.when(cond)
        def _():
            for j in range(LANE):
                halo(j, slot, y + step).wait_send()

    @pl.when(z > 0)
    def _():
        halo(0, LANE, y).wait_recv()

    @pl.when(z < SEG - 1)
    def _():
        halo(0, LANE + 1, y).wait_recv()


def scatter_kernel(parts, out, send, recv, own_sem):
    z, y, k = place()
    barrier = pltpu.get_barrier_semaphore()
    for j in range(LANE):
        @pl.when((y != z) | (k != j))
        def _():
            pl.semaphore_signal(barrier, inc=1, device_id=(y, z * LANE + j), device_id_type=MESH)
    pl.semaphore_wait(barrier, LANE - 1 + jnp.where(y != z, 1, 0))

    def main(j):
        return remote(parts.at[j], out.at[:, :, k], send.at[j], recv.at[k], y, z * LANE + j)

    own = pltpu.make_async_copy(parts.at[k], out.at[:, :, k], own_sem)
    for j in range(LANE):
        @pl.when((y != z) | (k != j))
        def _():
            main(j).start()

    @pl.when(y == z)
    def _():
        own.start()

    for j in range(LANE):
        @pl.when((y != z) | (k != j))
        def _():
            main(j).wait_send()
            remote(parts.at[j], out.at[:, :, j], send.at[j], recv.at[j], y, z * LANE + j).wait_recv()

    @pl.when(y == z)
    def _():
        own.wait()


def work_kernel(
    coef, ids, bx, ux, eb, eu, t5g, b_in, b_gain, b_head, u_in, u_gain, u_head,
    text_h, bkv_h, ukv_h, btime_h, bconv_h, bq_h, bo_h, utime_h, uconv_h, uq_h, uo_h, noise_h,
    early, parts,
    text_v, kv_w, btime_v, bconv_v, bq_v, bo_v, utime_v, uconv_v, uq_v, uo_v, noise_v,
    ctx, kv, taps, hid, query, att, x8b, x8u, rows8, aug8, gcol, wq_t, wo_t, wh_t, conv_t,
    kcat, vcat, mask_row, mask_col, head8, x2, hid3, act3, c2, sems,
):
    z, y, k = place()
    p = y * LANE + k

    copies = [
        pltpu.make_async_copy(src, dst, sems.at[n])
        for n, (src, dst) in enumerate(
            [
                (utime_h, utime_v), (uq_h, uq_v), (uo_h, uo_v), (uconv_h, uconv_v), (btime_h, btime_v),
                (bconv_h, bconv_v), (text_h, text_v),
            ]
            + [(bkv_h.at[:, 256 * n : 256 * n + 256], kv_w.at[n]) for n in range(4)]
            + [(ukv_h.at[n], kv_w.at[4 + n]) for n in range(2)]
            + [(bq_h, bq_v), (bo_h, bo_v), (noise_h, noise_v)]
        )
    ]
    for copy in copies:
        copy.start()
    at = dict(utime=0, uq=1, uo=2, uconv=3, btime=4, bconv=5, text=6, kv=7, bq=13, bo=14, noise=15)

    lane128 = iota((128, 128), 1)
    sub128 = iota((128, 128), 0)
    for m in range(2):
        x8b[m] = jnp.zeros((8, 1024), F32)
        x8u[m] = jnp.zeros((8, 1024), F32)
        x8b[m, 0:3, :] = bx[m].astype(F32)
        x8u[m, 0:3, :] = ux[m].astype(F32)
        row = jnp.where(ids[m, pl.ds(p, 1), :] != 0, 0.0, -1e30)
        mask_row[m, :, 0:128] = row
        mask_row[m, :, 128:256] = row
        rows8[...] = jnp.broadcast_to(row, (8, 128))
        column = jnp.transpose(rows8[...])[:, 0:1]
        mask_col[m] = jnp.broadcast_to(column, (128, 128))
    head8[...] = jnp.zeros_like(head8)
    head8[0:3, :] = b_head[...].astype(F32)

    for n in range(4):
        copies[n].wait()
    for s in range(2):
        emb = dot(eu[...].astype(BF16), utime_v[s])
        for m in range(2):
            aug8[0:6, :] = u_in[s].astype(F32)
            one = emb[2 * s + m : 2 * s + m + 1, :]
            high = one.astype(BF16).astype(F32)
            aug8[6:7, :] = high
            aug8[7:8, :] = one - high
            x8 = jnp.transpose(aug8[...]).astype(BF16)
            gcol[2 + 2 * s + m, :, 0:8] = x8.astype(F32)
        rows8[...] = jnp.zeros((8, 128), F32)
        rows8[0:3, :] = u_gain[s]
        turned = jnp.transpose(rows8[...])
        gcol[s] = jnp.broadcast_to(turned[:, 0:1] * 0.5, (128, 128))
        wq_t[s] = jnp.transpose(uq_v[s].astype(F32) * (turned[:, 1:2] * SCALE)).astype(BF16)
        wo_t[s] = jnp.transpose(uo_v[s].astype(F32)).astype(BF16)
        rows8[...] = jnp.zeros((8, 128), F32)
        rows8[0:3, :] = u_head[s].astype(F32) * u_gain[s, 2:3, :]
        wh_t[s] = rows8[...].astype(BF16)
        for tap in range(9):
            conv_t[s, :, 128 * tap : 128 * tap + 128] = jnp.transpose(uconv_v[s, tap].astype(F32)).astype(BF16)

    copies[at["btime"]].wait()
    emb_b = dot(eb[...].astype(BF16), btime_v[...])
    w_in = b_in[...]
    for m in range(2):
        rolled = pltpu.roll(x8b[m], jnp.mod(32 - 256 * z, 1024), 1)
        own_t = jnp.transpose(rolled[:, 0:384])[0:320, :]
        blk_t = jnp.transpose(x8b[m, :, 0:384])[0:288, :].reshape(9, 32, 8)[:, 0:16, :].reshape(144, 8)
        pix = jnp.concatenate([own_t, blk_t], axis=0)[:, 0:3].astype(BF16)
        hidden = dot(pix, w_in) + emb_b[m : m + 1, :]
        scale = lax.rsqrt(jnp.mean(hidden * hidden, axis=-1, keepdims=True) + 1e-6)
        half = hidden * scale * (b_gain[0:1, :] * 0.5)
        active = half + half * jnp.tanh(half)
        hid[256 * m : 256 * m + 256, :] = hidden[32:288]
        hid[512 + 64 * m : 576 + 64 * m, :] = hidden[320:464].reshape(9, 16, 512)[0:8, 0:8].reshape(64, 512)
        own = active[0:320]
        line = iota((320, 1), 0)
        gone = ((line < 32) & (z == 0)) | ((line >= 288) & (z == SEG - 1))
        own = jnp.where(gone, 0.0, own)
        blk = active[320:464]
        col = line % 32
        bcol = iota((144, 1), 0) % 16
        for b in range(3):
            if b == 0:
                mine = jnp.where(col == 0, 0.0, pltpu.roll(own, 1, 0))
                near = jnp.where(bcol == 0, 0.0, pltpu.roll(blk, 1, 0))
            elif b == 1:
                mine, near = own, blk
            else:
                mine = jnp.where(col == 31, 0.0, pltpu.roll(own, 319, 0))
                near = pltpu.roll(blk, 143, 0)
            mine = mine.astype(BF16)
            near = near.reshape(9, 16, 512)[:, 0:8].reshape(72, 512)
            near = jnp.concatenate([jnp.zeros((8, 512), F32), near], axis=0)
            for a in range(3):
                taps[3 * a + b, 256 * m : 256 * m + 256, :] = mine[32 * a : 32 * a + 256]
                taps[3 * a + b, 512 + 64 * m : 576 + 64 * m, :] = near[8 * a : 8 * a + 64].astype(BF16)

    copies[at["bconv"]].wait()

    def conv_step(tap, carry):
        hid[...] += dot(taps[tap], bconv_v[tap])
        return carry

    lax.fori_loop(0, 9, conv_step, 0)

    copies[at["text"]].wait()

    def norm_step(i, carry):
        at_row = pl.multiple_of(i * 32, 32)
        states = text_v[pl.ds(at_row, 32), :].astype(F32)
        scale = lax.rsqrt(jnp.mean(states * states, axis=-1, keepdims=True) + 1e-6)
        ctx[pl.ds(at_row, 32), :] = (states * scale * t5g[...]).astype(BF16)
        return carry

    lax.fori_loop(0, 8, norm_step, 0)
    for n in range(6):
        copies[at["kv"] + n].wait()
        kv[:, 256 * n : 256 * n + 256] = dot(ctx[...], kv_w[n]).astype(BF16)

    for s in range(2):
        for m in range(2):
            key = kv[128 * m : 128 * m + 128, 1024 + 256 * s : 1152 + 256 * s]
            val = jnp.transpose(kv[128 * m : 128 * m + 128, 1152 + 256 * s : 1280 + 256 * s].astype(F32)).astype(BF16)
            zero = jnp.zeros_like(key)
            kcat[2 * s + m, 0:128, :] = jnp.where(lane128 < 64, key, zero)
            kcat[2 * s + m, 128:256, :] = jnp.where(lane128 < 64, zero, key)
            vcat[2 * s + m, 0:128, 0:128] = jnp.where(sub128 < 64, val, zero)
            vcat[2 * s + m, 0:128, 128:256] = jnp.where(sub128 < 64, zero, val)
            head_of = iota((16, 256), 1) // 128
            vcat[2 * s + m, 128:144, :] = (head_of == iota((16, 256), 0)).astype(F32).astype(BF16)

    copies[at["bq"]].wait()
    copies[at["bo"]].wait()
    h2 = hid[...]
    scale = lax.rsqrt(jnp.mean(h2 * h2, axis=-1, keepdims=True) + 1e-6)
    query[...] = (dot((h2 * scale * b_gain[1:2, :]).astype(BF16), bq_v[...]) * SCALE).astype(BF16)
    for m in range(2):
        for pair in range(4):
            lo = 128 * pair
            key = kv[128 * m : 128 * m + 128, lo : lo + 128]
            val = kv[128 * m : 128 * m + 128, 512 + lo : 640 + lo]
            zero = jnp.zeros_like(key)
            keys = jnp.concatenate([jnp.where(lane128 < 64, key, zero), jnp.where(lane128 < 64, zero, key)], axis=0)
            vals = jnp.concatenate([jnp.where(lane128 < 64, val, zero), jnp.where(lane128 < 64, zero, val)], axis=0)
            ones = ((iota((256, 128), 0) < 128) == (iota((256, 128), 1) < 64)).astype(F32).astype(BF16)
            vals = jnp.concatenate([vals, ones], axis=1)
            q = jnp.concatenate(
                [query[256 * m : 256 * m + 256, lo : lo + 128], query[512 + 64 * m : 576 + 64 * m, lo : lo + 128]], axis=0
            )
            score = dot_nt(q, keys) + mask_row[m]
            left, right = score[:, 0:128], score[:, 128:256]
            left = jnp.exp2(left - jnp.max(left, axis=-1, keepdims=True))
            right = jnp.exp2(right - jnp.max(right, axis=-1, keepdims=True))
            mixed = dot(jnp.concatenate([left, right], axis=1).astype(BF16), vals)
            mixed = (mixed[:, 0:128] / mixed[:, 128:256]).astype(BF16)
            att[256 * m : 256 * m + 256, lo : lo + 128] = mixed[0:256]
            att[512 + 64 * m : 576 + 64 * m, lo : lo + 128] = mixed[256:320]
    h3 = hid[...] + dot(att[...], bo_v[...])
    scale = lax.rsqrt(jnp.mean(h3 * h3, axis=-1, keepdims=True) + 1e-6)
    eps = dot_nt(head8[...].astype(BF16), (h3 * scale * b_gain[2:3, :]).astype(BF16))

    def step_of(noisy, eps, c0, c1, c2_, c3):
        clean = jnp.clip((noisy - c0 * eps) * c1, -1.0, 1.0)
        return clean, c2_ * clean + c3 * eps

    def coefs(s, m):
        return tuple(coef[(2 * s + m) * 4 + n] for n in range(4))

    pick_k, pick_l = iota((256, 128), 0), iota((256, 128), 1)
    noisy = jnp.zeros((8, 128), F32)
    for m in range(2):
        whole = pltpu.roll(x8b[m], jnp.mod(0 - 256 * z, 1024), 1)[:, 0:256]
        _, prior = step_of(whole, eps[:, 256 * m : 256 * m + 256], *coefs(0, m))
        early[0, m] = prior
        spot = pick_l - 64 * m
        sel = (spot >= 0) & (spot < 64) & (pick_k // 32 == spot // 8) & (pick_k % 32 == spot % 8)
        noisy += dot(x8b[m, :, 0:256].astype(BF16), sel.astype(F32).astype(BF16))
    first_half = iota((8, 128), 1) < 64
    mixed_coefs = tuple(jnp.where(first_half, a, b) for a, b in zip(coefs(0, 0), coefs(0, 1)))
    region, _ = step_of(noisy, eps[:, 512:640], *mixed_coefs)
    region = region.astype(BF16)

    def back(s, m, h2, width):
        sm = 2 * s + m
        scale = lax.rsqrt(jnp.sum(h2 * h2, axis=0, keepdims=True) * (1.0 / 128.0) + 1e-6)
        q = (dot(wq_t[s], h2.astype(BF16)) * scale).astype(BF16)
        score = dot(kcat[sm], q)
        mask = jnp.concatenate([mask_col[m]] * (width // 128), axis=1)
        left, right = score[0:128] + mask, score[128:256] + mask
        left = jnp.exp2(left - jnp.max(left, axis=0, keepdims=True)).astype(BF16)
        right = jnp.exp2(right - jnp.max(right, axis=0, keepdims=True)).astype(BF16)
        mixed = dot(vcat[sm], jnp.concatenate([left, right], axis=0))
        top = mixed[0:64] * (1.0 / mixed[128:129])
        bottom = mixed[64:128] * (1.0 / mixed[129:130])
        h3 = h2 + dot(wo_t[s], jnp.concatenate([top, bottom], axis=0).astype(BF16))
        scale = lax.rsqrt(jnp.sum(h3 * h3, axis=0, keepdims=True) * (1.0 / 128.0) + 1e-6)
        return dot(wh_t[s], h3.astype(BF16)) * scale

    def activate(hidden, s, width):
        scale = lax.rsqrt(jnp.sum(hidden * hidden, axis=0, keepdims=True) * (1.0 / 128.0) + 1e-6)
        gain = jnp.concatenate([gcol[s]] * (width // 128), axis=1)
        half = hidden * scale * gain
        return half + half * jnp.tanh(half)

    lanes = iota((1, 384), 1)
    row_of = 8 * z - 2 + lanes // 32
    col_of = lanes % 32
    inside = (row_of >= 0) & (row_of < 32)
    spread_k = iota((128, 384), 0)
    spread_l = iota((128, 384), 1)
    spread_at = ((8 * z - 2 + spread_l // 32 + 4) // 4 - 1) * 8 + (spread_l % 32) // 4
    for m in range(2):
        x = pltpu.roll(x8u[m], jnp.mod(64 - 256 * z, 1024), 1)[:, 0:384]
        sel = (spread_k == spread_at + 64 * m) & (spread_at >= 0) & (spread_at < 64)
        cond = dot(region, sel.astype(F32).astype(BF16))
        which = iota((8, 384), 0)
        cond = pltpu.roll(cond, 3, 0)
        x8 = jnp.where(which < 3, x, jnp.where(which < 6, cond, 1.0))
        hidden = dot(gcol[2 + m, :, 0:8].astype(BF16), x8.astype(BF16))
        active = jnp.where(inside, activate(hidden, 0, 384), 0.0)
        stack = [
            jnp.where(col_of == 0, 0.0, pltpu.roll(active, 1, 1)),
            active,
            jnp.where(col_of == 31, 0.0, pltpu.roll(active, 383, 1)),
        ]
        stack = [pltpu.roll(one, 32, 1) for one in stack] + stack + [pltpu.roll(one, 352, 1) for one in stack]
        stack = jnp.concatenate([one.astype(BF16) for one in stack], axis=0)
        h2 = hidden + dot(conv_t[0], stack)
        eps = back(0, m, h2, 384)
        clean, prior = step_of(x, eps, *coefs(1, m))
        early[1, m] = pltpu.roll(prior, 320, 1)[:, 0:256]
        clean = clean.astype(BF16)
        pick_k, pick_l = iota((384, 128), 0), iota((384, 128), 1)

        def rows_at(first):
            sel = (pick_k // 32 == first + 2 * (pick_l // 32)) & (pick_k % 32 == pick_l % 32)
            return dot(clean, sel.astype(F32).astype(BF16))

        x2[m] = jnp.ones((34 * 8, 128), F32)
        even, odd = rows_at(2), rows_at(3)
        above, below = rows_at(1), rows_at(4)
        for c in range(3):
            x2[m, pl.ds(8 + 3 + c, 16, 8), :] = jnp.broadcast_to(even[c : c + 1], (16, 128))
            x2[m, pl.ds(8 * 17 + 3 + c, 16, 8), :] = jnp.broadcast_to(odd[c : c + 1], (16, 128))
            x2[m, 3 + c : 4 + c, :] = above[c : c + 1]
            x2[m, 33 * 8 + 3 + c : 33 * 8 + 4 + c, :] = below[c : c + 1]

    copies[at["noise"]].wait()

    @pl.when(z == 0)
    def _():
        noise_v[8] = jnp.zeros((2, 3, 16, 32), BF16)

    @pl.when(z == SEG - 1)
    def _():
        noise_v[9] = jnp.zeros((2, 3, 16, 32), BF16)

    def spot(g):
        return (iota((32, 128), 0) + 32 * g == iota((32, 128), 1)).astype(F32).astype(BF16)

    lane1 = iota((1, 128), 1)
    for m in range(2):
        total = jnp.zeros((96, 128), F32)
        for g in range(4):
            pieces = jnp.concatenate([noise_v[2 * g, m], noise_v[2 * g + 1, m]], axis=1).reshape(96, 32)
            total += dot(pieces, spot(g))
        top = dot(noise_v[8, m].reshape(48, 32), spot(0))
        low = dot(noise_v[9, m].reshape(48, 32), spot(3))
        for c in range(3):
            one = total[32 * c : 32 * c + 32]
            x2[m, pl.ds(8 + c, 32, 8), :] = one
            x2[m, c : c + 1, :] = jnp.where(lane1 < 32, top[16 * c + 15 : 16 * c + 16], pltpu.roll(one[31:32], 32, 1))
            x2[m, 33 * 8 + c : 33 * 8 + c + 1, :] = jnp.where(
                lane1 >= 96, low[16 * c : 16 * c + 1], pltpu.roll(one[0:1], 96, 1)
            )

    lane2 = iota((1, 256), 1) % 128
    col2 = lane2 % 32
    for m in range(2):
        def front_step(n, carry):
            t = n * 2
            pair = x2[m, pl.ds(pl.multiple_of(t * 8, 16), 16), :]
            x8 = jnp.concatenate([pair[0:8], pair[8:16]], axis=1).astype(BF16)
            hidden = dot(gcol[4 + m, :, 0:8].astype(BF16), x8)
            hid3[t] = hidden[:, 0:128]
            hid3[t + 1] = hidden[:, 128:256]
            tile = t + iota((1, 256), 1) // 128
            gone = ((tile == 0) & (lane2 < 32) & (z == 0)) | ((tile == 33) & (lane2 >= 96) & (z == SEG - 1))
            active = jnp.where(gone, 0.0, activate(hidden, 1, 256))
            for h in range(2):
                one = active[:, 128 * h : 128 * h + 128]
                act3[t + h, 0:128] = jnp.where(col2[:, 0:128] == 0, 0.0, pltpu.roll(one, 1, 1)).astype(BF16)
                act3[t + h, 128:256] = one.astype(BF16)
                act3[t + h, 256:384] = jnp.where(col2[:, 0:128] == 31, 0.0, pltpu.roll(one, 127, 1)).astype(BF16)
            return carry

        lax.fori_loop(0, 17, front_step, 0)

        def back_step(n, carry):
            i = n * STEPS
            tiles = [act3[i + e] for e in range(STEPS + 2)]
            stack = jnp.concatenate(
                [jnp.concatenate(tiles[a : a + STEPS], axis=1) for a in range(3)], axis=0
            )
            h2 = jnp.concatenate([hid3[i + 1 + e] for e in range(STEPS)], axis=1) + dot(conv_t[1], stack)
            eps = back(1, m, h2, 128 * STEPS)
            rows = x2[m, pl.ds(pl.multiple_of((i + 1) * 8, 8), 8 * STEPS), :]
            noisy = jnp.concatenate([rows[8 * e : 8 * e + 8] for e in range(STEPS)], axis=1)
            clean, prior = step_of(noisy, eps, *coefs(2, m))
            for e in range(STEPS):
                spot_at = pl.ds(pl.multiple_of((i + e) * 8, 8), 8)
                c2[0, m, spot_at, :] = clean[:, 128 * e : 128 * e + 128]
                c2[1, m, spot_at, :] = prior[:, 128 * e : 128 * e + 128]
            return carry

        lax.fori_loop(0, 32 // STEPS, back_step, 0)

    everything = jnp.concatenate(
        [c2[o, m, pl.ds(c, 32, 8), :] for o in range(2) for m in range(2) for c in range(3)], axis=0
    ).astype(BF16)
    for g in range(4):
        sel = (iota((128, 32), 0) == iota((128, 32), 1) + 32 * g).astype(F32).astype(BF16)
        piece = dot(everything, sel).astype(BF16).reshape(2, 2, 3, 32, 32)
        parts[2 * g] = piece[:, :, :, 0:16]
        parts[2 * g + 1] = piece[:, :, :, 16:32]


def alpha_bar(step):
    frac = (step.astype(F32) / 1000.0 + 0.008) / 1.008
    return jnp.cos(frac * (math.pi / 2)) ** 2


def time_code(step, half):
    freqs = jnp.exp(-math.log(10000.0) * jnp.arange(half, dtype=F32) / half)
    angle = step.astype(F32)[:, None] * freqs
    return jnp.concatenate([jnp.sin(angle), jnp.cos(angle)], axis=1).astype(BF16).astype(F32)


def shards(
    text_states, token_ids, step_ids, base_noise, upscale_noise, final_noise, t5_gain,
    base_keyval, upscale_keyval, base_input, base_time, base_gain, base_conv, base_query,
    base_output, base_head, upscale_input, upscale_time, upscale_gain, upscale_conv,
    upscale_query, upscale_output, upscale_head,
):
    steps = step_ids.reshape(-1)
    level, earlier = alpha_bar(steps), alpha_bar(steps - 50)
    coef = jnp.stack(
        [jnp.sqrt(1.0 - level), lax.rsqrt(level), jnp.sqrt(earlier), jnp.sqrt(1.0 - earlier)], axis=1
    ).reshape(-1)
    code_base = jnp.pad(time_code(step_ids[0], 256), ((0, 6), (0, 0)))
    code_up = jnp.pad(time_code(steps[2:], 64), ((0, 4), (0, 0)))

    remote_params = dict(has_side_effects=True)
    got = pl.pallas_call(
        gather_kernel,
        out_shape=jax.ShapeDtypeStruct((LANE + 2, 2, 3, 16, 32), BF16),
        in_specs=[ANY],
        out_specs=ANY,
        scratch_shapes=[
            pltpu.SemaphoreType.DMA((LANE,)),
            pltpu.SemaphoreType.DMA((LANE + 2,)),
            pltpu.SemaphoreType.DMA((LANE,)),
            pltpu.SemaphoreType.DMA,
        ],
        compiler_params=pltpu.CompilerParams(collective_id=0, **remote_params),
        name="noise_in",
    )(final_noise)

    early, parts = pl.pallas_call(
        work_kernel,
        out_shape=(
            jax.ShapeDtypeStruct((2, 2, 8, 256), F32),
            jax.ShapeDtypeStruct((LANE, 2, 2, 3, 16, 32), BF16),
        ),
        in_specs=[SMEM] + [VMEM] * 12 + [ANY] * 12,
        out_specs=(VMEM, VMEM),
        scratch_shapes=[
            pltpu.VMEM((256, 4096), BF16),
            pltpu.VMEM((6, 4096, 256), BF16),
            pltpu.VMEM((512, 512), BF16),
            pltpu.VMEM((9, 512, 512), BF16),
            pltpu.VMEM((512, 512), BF16),
            pltpu.VMEM((512, 512), BF16),
            pltpu.VMEM((2, 128, 128), BF16),
            pltpu.VMEM((2, 9, 128, 128), BF16),
            pltpu.VMEM((2, 128, 128), BF16),
            pltpu.VMEM((2, 128, 128), BF16),
            pltpu.VMEM((LANE + 2, 2, 3, 16, 32), BF16),
            pltpu.VMEM((256, 4096), BF16),
            pltpu.VMEM((256, 1536), BF16),
            pltpu.VMEM((9, 640, 512), BF16),
            pltpu.VMEM((640, 512), F32),
            pltpu.VMEM((640, 512), BF16),
            pltpu.VMEM((640, 512), BF16),
            pltpu.VMEM((2, 8, 1024), F32),
            pltpu.VMEM((2, 8, 1024), F32),
            pltpu.VMEM((8, 128), F32),
            pltpu.VMEM((8, 128), F32),
            pltpu.VMEM((6, 128, 128), F32),
            pltpu.VMEM((2, 128, 128), BF16),
            pltpu.VMEM((2, 128, 128), BF16),
            pltpu.VMEM((2, 8, 128), BF16),
            pltpu.VMEM((2, 128, 1152), BF16),
            pltpu.VMEM((4, 256, 128), BF16),
            pltpu.VMEM((4, 144, 256), BF16),
            pltpu.VMEM((2, 1, 256), F32),
            pltpu.VMEM((2, 128, 128), F32),
            pltpu.VMEM((8, 512), F32),
            pltpu.VMEM((2, 272, 128), F32),
            pltpu.VMEM((34, 128, 128), F32),
            pltpu.VMEM((34, 384, 128), BF16),
            pltpu.VMEM((2, 2, 256, 128), F32),
            pltpu.SemaphoreType.DMA((16,)),
        ],
        compiler_params=pltpu.CompilerParams(vmem_limit_bytes=56 * 1024 * 1024),
        name="sections",
    )(
        coef, token_ids, base_noise[:, 0], upscale_noise[:, 0], code_base, code_up, t5_gain[None],
        base_input, base_gain, base_head.T, upscale_input, upscale_gain, upscale_head.transpose(0, 2, 1),
        text_states.reshape(256, 4096), base_keyval, upscale_keyval, base_time, base_conv, base_query, base_output,
        upscale_time, upscale_conv, upscale_query, upscale_output, got,
    )

    final_states = pl.pallas_call(
        scatter_kernel,
        out_shape=jax.ShapeDtypeStruct((2, 2, LANE, 3, 16, 32), BF16),
        in_specs=[ANY],
        out_specs=ANY,
        scratch_shapes=[
            pltpu.SemaphoreType.DMA((LANE,)),
            pltpu.SemaphoreType.DMA((LANE,)),
            pltpu.SemaphoreType.DMA,
        ],
        compiler_params=pltpu.CompilerParams(collective_id=1, **remote_params),
        name="results_out",
    )(parts)
    early_states = early[:, :, None, 0:3, :].astype(BF16)
    return early_states, final_states


def solution(mesh):
    placed = [P() for _ in range(23)]
    placed[0] = placed[3] = placed[4] = P(None, "space", None, None)
    placed[5] = P(None, None, None, "space", None)
    return jax.shard_map(
        shards,
        mesh=mesh,
        in_specs=tuple(placed),
        out_specs=(
            P(None, None, "space", None, "segment"),
            P(None, None, "segment", None, "space", None),
        ),
        check_vma=False,
    )
```

```python
import functools
import math

import jax
import jax.numpy as jnp
from jax import lax
from jax.experimental import pallas as pl
from jax.experimental.pallas import tpu as pltpu
from jax.sharding import PartitionSpec as P

MESH = pl.DeviceIdType.MESH
ANY = pl.BlockSpec(memory_space=pl.ANY)
VMEM = pl.BlockSpec(memory_space=pltpu.VMEM)
SMEM = pl.BlockSpec(memory_space=pltpu.SMEM)
F32, BF16 = jnp.float32, jnp.bfloat16
LOG2E = 1.4426950408889634
SCALE = 0.125 * LOG2E
SEG, LANE = 4, 8

STEPS = 16


def dot(a, b):
    return jnp.dot(a, b, preferred_element_type=F32)


def dot_nt(a, b):
    return lax.dot_general(a, b, (((1,), (1,)), ((), ())), preferred_element_type=F32)


def iota(shape, dim):
    return lax.broadcasted_iota(jnp.int32, shape, dim)


def place():
    z = lax.axis_index("segment")
    p = lax.axis_index("space")
    return z, p // LANE, p % LANE


def remote(src, dst, send, recv, z, p):
    return pltpu.make_async_remote_copy(
        src_ref=src, dst_ref=dst, send_sem=send, recv_sem=recv, device_id=(z, p), device_id_type=MESH
    )


def each_other(z, y, k, body):
    for j in range(LANE):
        @pl.when((y != z) | (k != j))
        def _():
            body(j)


def step_kernel(
    steps, ids, bx, ux, t5g, b_in, b_gain, b_head, u_in, u_gain, u_head,
    noise_h, text_h, bkv_h, ukv_h, btime_h, bconv_h, bq_h, bo_h, utime_h, uconv_h, uq_h, uo_h,
    early, out,
    text_v, kv_w, btime_v, bconv_v, bq_v, bo_v, utime_v, uconv_v, uq_v, uo_v, noise_v,
    ctx, kv, taps, hid, query, att, x8b, x8u, rows8, aug8, gcol, wq_t, wo_t, wh_t, conv_t,
    kcat, vcat, mask_row, mask_col, head8, x2, hid3, act3, c2, early_v,
    snd, snd_b, rcv, snd2, rcv2, sems, send, recv, halo_send, send2, recv2,
):
    z, y, k = place()
    p = y * LANE + k

    barrier = pltpu.get_barrier_semaphore()

    def hello(z_to, p_to):
        pl.semaphore_signal(barrier, inc=1, device_id=(z_to, p_to), device_id_type=MESH)

    each_other(z, y, k, lambda j: hello(y, z * LANE + j))

    @pl.when(z > 0)
    def _():
        hello(y, z * LANE - 1)

    @pl.when(z < SEG - 1)
    def _():
        hello(y, z * LANE + LANE)

    copies = [
        pltpu.make_async_copy(src, dst, sems.at[n])
        for n, (src, dst) in enumerate(
            [
                (noise_h.at[:, pl.ds(z * LANE, LANE)], noise_v),
                (utime_h, utime_v), (uq_h, uq_v), (uo_h, uo_v), (uconv_h, uconv_v), (btime_h, btime_v),
                (text_h, text_v), (bconv_h, bconv_v),
            ]
            + [(bkv_h.at[:, 512 * n : 512 * n + 512], kv_w.at[n]) for n in range(2)]
            + [(ukv_h.at[n], kv_w.at[2, :, 256 * n : 256 * n + 256]) for n in range(2)]
            + [(bq_h, bq_v), (bo_h, bo_v)]
        )
    ]
    for copy in copies:
        copy.start()
    at = dict(noise=0, utime=1, uq=2, uo=3, uconv=4, btime=5, text=6, bconv=7, kv=8, bq=12, bo=13)

    copies[at["noise"]].wait()
    packed = jnp.zeros((LANE * 24, 128), F32)
    for m in range(2):
        rows = noise_v[m].astype(F32)
        for half in range(2):
            group = 2 * m + half
            place_at = (iota((32, 128), 0) + 32 * group == iota((32, 128), 1)).astype(F32).astype(BF16)
            packed += dot(rows[:, :, 8 * half : 8 * half + 8, :].reshape(LANE * 24, 32).astype(BF16), place_at)
    snd[:, 0:24, :] = packed.reshape(LANE, 24, 128)
    snd[:, 24:32, :] = jnp.zeros((LANE, 8, 128), F32)
    snd_b[...] = snd[...].astype(BF16)

    lower = (k == LANE - 1) & (y < SEG - 1)
    upper = (k == 0) & (y > 0)
    extra = jnp.where(lower | upper, LANE, 0)
    pl.semaphore_wait(barrier, LANE - 1 + jnp.where(y != z, 1, 0) + extra)

    def noise_to(j, slot):
        return remote(snd_b.at[j], rcv.at[slot], send.at[j], recv.at[slot], y, z * LANE + j)

    def halo_to(j, slot, to):
        return remote(snd_b.at[j], rcv.at[slot], halo_send.at[j], recv.at[slot], to, z * LANE + j)

    each_other(z, y, k, lambda j: noise_to(j, k).start())
    for cond, slot, step in ((lower, LANE, 1), (upper, LANE + 1, -1)):
        @pl.when(cond)
        def _():
            for j in range(LANE):
                halo_to(j, slot, y + step).start()

    @pl.when(y == z)
    def _():
        rcv[k] = snd_b[k]

    lane128 = iota((128, 128), 1)
    sub128 = iota((128, 128), 0)
    for m in range(2):
        x8b[m] = jnp.zeros((8, 1024), F32)
        x8u[m] = jnp.zeros((8, 1024), F32)
        for c in range(3):
            x8b[m, c : c + 1, :] = bx[c].astype(F32)[m : m + 1]
            x8u[m, c : c + 1, :] = ux[c].astype(F32)[m : m + 1]
        row = jnp.where(ids[m, pl.ds(p, 1), :] != 0, 0.0, -1e30)
        mask_row[m, :, 0:128] = row
        mask_row[m, :, 128:256] = row
        rows8[...] = jnp.broadcast_to(row, (8, 128))
        column = jnp.transpose(rows8[...])[:, 0:1]
        mask_col[m] = jnp.broadcast_to(column, (128, 128))
    head8[...] = jnp.zeros_like(head8)
    head8[0:3, :] = b_head[...].astype(F32)

    def code(width, first):
        row, lane = iota((8, width), 0), iota((8, width), 1)
        step = jnp.zeros((8, width), F32)
        for s in range(2):
            for m in range(2):
                section = min(first + s, 2)
                step = jnp.where(row == 2 * s + m, steps[m, section].astype(F32), step)
        half = width // 2
        angle = step * jnp.exp((-math.log(10000.0) / half) * (lane % half).astype(F32))
        return jnp.where(lane < half, jnp.sin(angle), jnp.cos(angle)).astype(BF16)

    def coefs(s, m):
        step = jnp.full((8, 128), steps[m, s].astype(F32))

        def alpha(at_step):
            return jnp.cos((at_step / 1000.0 + 0.008) * (math.pi / 2 / 1.008)) ** 2

        level, earlier = alpha(step), alpha(step - 50.0)
        return jnp.sqrt(1.0 - level), 1.0 / jnp.sqrt(level), jnp.sqrt(earlier), jnp.sqrt(1.0 - earlier)

    for n in range(1, 5):
        copies[n].wait()
    code_up = code(128, 1)
    code_base = code(512, 0)
    for s in range(2):
        emb = dot(code_up, utime_v[s])
        for m in range(2):
            for c in range(6):
                aug8[c : c + 1, :] = u_in[c].astype(F32)[s : s + 1]
            one = emb[2 * s + m : 2 * s + m + 1, :]
            high = one.astype(BF16).astype(F32)
            aug8[6:7, :] = high
            aug8[7:8, :] = one - high
            x8 = jnp.transpose(aug8[...]).astype(BF16)
            gcol[2 + 2 * s + m, :, 0:8] = x8.astype(F32)
        rows8[...] = jnp.zeros((8, 128), F32)
        for c in range(3):
            rows8[c : c + 1, :] = u_gain[c, s : s + 1, :]
        turned = jnp.transpose(rows8[...])
        gcol[s] = jnp.broadcast_to(turned[:, 0:1] * 0.5, (128, 128))
        wq_t[s] = jnp.transpose(uq_v[s].astype(F32) * (turned[:, 1:2] * SCALE)).astype(BF16)
        wo_t[s] = jnp.transpose(uo_v[s].astype(F32)).astype(BF16)
        rows8[...] = jnp.zeros((8, 128), F32)
        for c in range(3):
            rows8[c : c + 1, :] = u_head[c].astype(F32)[s : s + 1] * u_gain[2, s : s + 1, :]
        wh_t[s] = rows8[...].astype(BF16)
        for tap in range(9):
            conv_t[s, :, 128 * tap : 128 * tap + 128] = jnp.transpose(uconv_v[s, tap].astype(F32)).astype(BF16)

    copies[at["btime"]].wait()
    emb_b = dot(code_base, btime_v[...])
    w_in = b_in[...]
    for m in range(2):
        rolled = pltpu.roll(x8b[m], jnp.mod(32 - 256 * z, 1024), 1)
        own_t = jnp.transpose(rolled[:, 0:384])[0:320, :]
        blk_t = jnp.transpose(x8b[m, :, 0:384])[0:288, :].reshape(9, 32, 8)[:, 0:16, :].reshape(144, 8)
        pix = jnp.concatenate([own_t, blk_t], axis=0)[:, 0:3].astype(BF16)
        hidden = dot(pix, w_in) + emb_b[m : m + 1, :]
        scale = lax.rsqrt(jnp.mean(hidden * hidden, axis=-1, keepdims=True) + 1e-6)
        half = hidden * scale * (b_gain[0:1, :] * 0.5)
        active = half + half * jnp.tanh(half)
        hid[256 * m : 256 * m + 256, :] = hidden[32:288]
        hid[512 + 64 * m : 576 + 64 * m, :] = hidden[320:464].reshape(9, 16, 512)[0:8, 0:8].reshape(64, 512)
        own = active[0:320]
        line = iota((320, 1), 0)
        gone = ((line < 32) & (z == 0)) | ((line >= 288) & (z == SEG - 1))
        own = jnp.where(gone, 0.0, own)
        blk = active[320:464]
        col = line % 32
        bcol = iota((144, 1), 0) % 16
        for b in range(3):
            if b == 0:
                mine = jnp.where(col == 0, 0.0, pltpu.roll(own, 1, 0))
                near = jnp.where(bcol == 0, 0.0, pltpu.roll(blk, 1, 0))
            elif b == 1:
                mine, near = own, blk
            else:
                mine = jnp.where(col == 31, 0.0, pltpu.roll(own, 319, 0))
                near = pltpu.roll(blk, 143, 0)
            mine = mine.astype(BF16)
            near = near.reshape(9, 16, 512)[:, 0:8].reshape(72, 512)
            near = jnp.concatenate([jnp.zeros((8, 512), F32), near], axis=0)
            for a in range(3):
                taps[a, 256 * m : 256 * m + 256, 512 * b : 512 * b + 512] = mine[32 * a : 32 * a + 256]
                taps[a, 512 + 64 * m : 576 + 64 * m, 512 * b : 512 * b + 512] = near[8 * a : 8 * a + 64].astype(BF16)

    copies[at["text"]].wait()

    def norm_step(i, carry):
        at_row = pl.multiple_of(i * 64, 64)
        states = text_v[pl.ds(at_row, 64), :].astype(F32)
        scale = lax.rsqrt(jnp.mean(states * states, axis=-1, keepdims=True) + 1e-6)
        ctx[pl.ds(at_row, 64), :] = (states * scale * t5g[...]).astype(BF16)
        return carry

    lax.fori_loop(0, 4, norm_step, 0)
    copies[at["bconv"]].wait()

    def conv_step(tap, carry):
        hid[...] += dot(taps[tap], bconv_v[tap])
        return carry

    lax.fori_loop(0, 3, conv_step, 0)

    for n in range(3):
        copies[at["kv"] + n].wait()
        if n == 2:
            copies[at["kv"] + 3].wait()
        kv[:, 512 * n : 512 * n + 512] = dot(ctx[...], kv_w[n]).astype(BF16)

    for s in range(2):
        for m in range(2):
            key = kv[128 * m : 128 * m + 128, 1024 + 256 * s : 1152 + 256 * s]
            val = jnp.transpose(kv[128 * m : 128 * m + 128, 1152 + 256 * s : 1280 + 256 * s].astype(F32)).astype(BF16)
            zero = jnp.zeros_like(key)
            kcat[2 * s + m, 0:128, :] = jnp.where(lane128 < 64, key, zero)
            kcat[2 * s + m, 128:256, :] = jnp.where(lane128 < 64, zero, key)
            vcat[2 * s + m, 0:128, 0:128] = jnp.where(sub128 < 64, val, zero)
            vcat[2 * s + m, 0:128, 128:256] = jnp.where(sub128 < 64, zero, val)
            head_of = iota((16, 256), 1) // 128
            vcat[2 * s + m, 128:144, :] = (head_of == iota((16, 256), 0)).astype(F32).astype(BF16)

    copies[at["bq"]].wait()
    copies[at["bo"]].wait()
    h2 = hid[...]
    scale = lax.rsqrt(jnp.mean(h2 * h2, axis=-1, keepdims=True) + 1e-6)
    query[...] = (dot((h2 * scale * b_gain[1:2, :]).astype(BF16), bq_v[...]) * SCALE).astype(BF16)
    for m in range(2):
        for pair in range(4):
            lo = 128 * pair
            key = kv[128 * m : 128 * m + 128, lo : lo + 128]
            val = kv[128 * m : 128 * m + 128, 512 + lo : 640 + lo]
            zero = jnp.zeros_like(key)
            keys = jnp.concatenate([jnp.where(lane128 < 64, key, zero), jnp.where(lane128 < 64, zero, key)], axis=0)
            vals = jnp.concatenate([jnp.where(lane128 < 64, val, zero), jnp.where(lane128 < 64, zero, val)], axis=0)
            ones = ((iota((256, 128), 0) < 128) == (iota((256, 128), 1) < 64)).astype(F32).astype(BF16)
            vals = jnp.concatenate([vals, ones], axis=1)
            q = jnp.concatenate(
                [query[256 * m : 256 * m + 256, lo : lo + 128], query[512 + 64 * m : 576 + 64 * m, lo : lo + 128]], axis=0
            )
            score = dot_nt(q, keys) + mask_row[m]
            left, right = score[:, 0:128], score[:, 128:256]
            left = jnp.exp2(left - jnp.max(left, axis=-1, keepdims=True))
            right = jnp.exp2(right - jnp.max(right, axis=-1, keepdims=True))
            mixed = dot(jnp.concatenate([left, right], axis=1).astype(BF16), vals)
            mixed = (mixed[:, 0:128] / mixed[:, 128:256]).astype(BF16)
            att[256 * m : 256 * m + 256, lo : lo + 128] = mixed[0:256]
            att[512 + 64 * m : 576 + 64 * m, lo : lo + 128] = mixed[256:320]
    h3 = hid[...] + dot(att[...], bo_v[...])
    scale = lax.rsqrt(jnp.mean(h3 * h3, axis=-1, keepdims=True) + 1e-6)
    eps = dot_nt(head8[...].astype(BF16), (h3 * scale * b_gain[2:3, :]).astype(BF16))

    def step_of(noisy, eps, c0, c1, c2_, c3):
        c0, c1, c2_, c3 = (jnp.concatenate([c] * (eps.shape[1] // 128), axis=1) for c in (c0, c1, c2_, c3))
        clean = jnp.clip((noisy - c0 * eps) * c1, -1.0, 1.0)
        return clean, c2_ * clean + c3 * eps

    pick_k, pick_l = iota((256, 128), 0), iota((256, 128), 1)
    noisy = jnp.zeros((8, 128), F32)
    for m in range(2):
        whole = pltpu.roll(x8b[m], jnp.mod(0 - 256 * z, 1024), 1)[:, 0:256]
        _, prior = step_of(whole, eps[:, 256 * m : 256 * m + 256], *coefs(0, m))
        for c in range(3):
            early_v[0, c, m : m + 1, :] = prior[c : c + 1]
        spot = pick_l - 64 * m
        sel = (spot >= 0) & (spot < 64) & (pick_k // 32 == spot // 8) & (pick_k % 32 == spot % 8)
        noisy += dot(x8b[m, :, 0:256].astype(BF16), sel.astype(F32).astype(BF16))
    first_half = iota((8, 128), 1) < 64
    mixed_coefs = tuple(jnp.where(first_half, a, b) for a, b in zip(coefs(0, 0), coefs(0, 1)))
    region, _ = step_of(noisy, eps[:, 512:640], *mixed_coefs)
    region = region.astype(BF16)

    def back(s, m, h2, width):
        sm = 2 * s + m
        scale = lax.rsqrt(jnp.sum(h2 * h2, axis=0, keepdims=True) * (1.0 / 128.0) + 1e-6)
        q = (dot(wq_t[s], h2.astype(BF16)) * scale).astype(BF16)
        score = dot(kcat[sm], q)
        mask = jnp.concatenate([mask_col[m]] * (width // 128), axis=1)
        left, right = score[0:128] + mask, score[128:256] + mask
        left = jnp.exp2(left - jnp.max(left, axis=0, keepdims=True)).astype(BF16)
        right = jnp.exp2(right - jnp.max(right, axis=0, keepdims=True)).astype(BF16)
        mixed = dot(vcat[sm], jnp.concatenate([left, right], axis=0))
        top = mixed[0:64] * (1.0 / mixed[128:129])
        bottom = mixed[64:128] * (1.0 / mixed[129:130])
        h3 = h2 + dot(wo_t[s], jnp.concatenate([top, bottom], axis=0).astype(BF16))
        scale = lax.rsqrt(jnp.sum(h3 * h3, axis=0, keepdims=True) * (1.0 / 128.0) + 1e-6)
        return dot(wh_t[s], h3.astype(BF16)) * scale

    def activate(hidden, s, width):
        scale = lax.rsqrt(jnp.sum(hidden * hidden, axis=0, keepdims=True) * (1.0 / 128.0) + 1e-6)
        gain = jnp.concatenate([gcol[s]] * (width // 128), axis=1)
        half = hidden * scale * gain
        return half + half * jnp.tanh(half)

    lanes = iota((1, 384), 1)
    row_of = 8 * z - 2 + lanes // 32
    col_of = lanes % 32
    inside = (row_of >= 0) & (row_of < 32)
    spread_k = iota((128, 384), 0)
    spread_l = iota((128, 384), 1)
    spread_at = ((8 * z - 2 + spread_l // 32 + 4) // 4 - 1) * 8 + (spread_l % 32) // 4
    for m in range(2):
        x = pltpu.roll(x8u[m], jnp.mod(64 - 256 * z, 1024), 1)[:, 0:384]
        sel = (spread_k == spread_at + 64 * m) & (spread_at >= 0) & (spread_at < 64)
        cond = dot(region, sel.astype(F32).astype(BF16))
        which = iota((8, 384), 0)
        cond = pltpu.roll(cond, 3, 0)
        x8 = jnp.where(which < 3, x, jnp.where(which < 6, cond, 1.0))
        hidden = dot(gcol[2 + m, :, 0:8].astype(BF16), x8.astype(BF16))
        active = jnp.where(inside, activate(hidden, 0, 384), 0.0)
        stack = [
            jnp.where(col_of == 0, 0.0, pltpu.roll(active, 1, 1)),
            active,
            jnp.where(col_of == 31, 0.0, pltpu.roll(active, 383, 1)),
        ]
        stack = [pltpu.roll(one, 32, 1) for one in stack] + stack + [pltpu.roll(one, 352, 1) for one in stack]
        stack = jnp.concatenate([one.astype(BF16) for one in stack], axis=0)
        h2 = hidden + dot(conv_t[0], stack)
        eps = back(0, m, h2, 384)
        clean, prior = step_of(x, eps, *coefs(1, m))
        prior = pltpu.roll(prior, 320, 1)[:, 0:256]
        for c in range(3):
            early_v[1, c, m : m + 1, :] = prior[c : c + 1]
        clean = clean.astype(BF16)
        pick_k, pick_l = iota((384, 128), 0), iota((384, 128), 1)

        def rows_at(first):
            sel = (pick_k // 32 == first + 2 * (pick_l // 32)) & (pick_k % 32 == pick_l % 32)
            return dot(clean, sel.astype(F32).astype(BF16))

        x2[m] = jnp.ones((34 * 8, 128), F32)
        even, odd = rows_at(2), rows_at(3)
        above, below = rows_at(1), rows_at(4)
        for c in range(3):
            x2[m, pl.ds(8 + 3 + c, 16, 8), :] = jnp.broadcast_to(even[c : c + 1], (16, 128))
            x2[m, pl.ds(8 * 17 + 3 + c, 16, 8), :] = jnp.broadcast_to(odd[c : c + 1], (16, 128))
            x2[m, 3 + c : 4 + c, :] = above[c : c + 1]
            x2[m, 33 * 8 + 3 + c : 33 * 8 + 4 + c, :] = below[c : c + 1]

    pass

    early[...] = early_v[...].astype(BF16)
    each_other(z, y, k, lambda j: noise_to(j, j).wait_recv())

    @pl.when(z > 0)
    def _():
        noise_to(0, LANE).wait_recv()

    @pl.when(z < SEG - 1)
    def _():
        noise_to(0, LANE + 1).wait_recv()

    @pl.when(z == 0)
    def _():
        rcv[LANE] = jnp.zeros((32, 128), BF16)

    @pl.when(z == SEG - 1)
    def _():
        rcv[LANE + 1] = jnp.zeros((32, 128), BF16)

    lane1 = iota((1, 128), 1)

    def regroup(value, source, target):
        by = 32 * (target - source) % 128
        return pltpu.roll(value, by, 1) if by else value

    blocks = [rcv[n].astype(F32)[0:24] for n in range(LANE + 2)]
    for m in range(2):
        edge = {}
        for h in range(2):
            for half in range(2):
                group = 2 * m + half
                total = regroup(blocks[h], group, 0)
                for g in range(1, 4):
                    total = jnp.where(lane1 // 32 == g, regroup(blocks[2 * g + h], group, g), total)
                edge[h, half] = total
                for c in range(3):
                    x2[m, pl.ds(8 * (1 + 16 * h + 8 * half) + c, 8, 8), :] = total[8 * c : 8 * c + 8]
        top = regroup(blocks[LANE], 2 * m + 1, 0)
        low = regroup(blocks[LANE + 1], 2 * m, 3)
        over = pltpu.roll(edge[1, 1], 32, 1)
        under = pltpu.roll(edge[0, 0], 96, 1)
        for c in range(3):
            x2[m, c : c + 1, :] = jnp.where(lane1 < 32, top, over)[8 * c + 7 : 8 * c + 8]
            x2[m, 33 * 8 + c : 33 * 8 + c + 1, :] = jnp.where(lane1 >= 96, low, under)[8 * c : 8 * c + 1]

    lane2 = iota((1, 256), 1) % 128
    col2 = lane2 % 32
    for m in range(2):
        FT = 17
        colf = iota((1, 128 * FT), 1) % 32
        for n in range(34 // FT):
            t = n * FT
            rows = x2[m, t * 8 : (t + FT) * 8, :]
            x8 = jnp.concatenate([rows[8 * e : 8 * e + 8] for e in range(FT)], axis=1).astype(BF16)
            hidden = dot(gcol[4 + m, :, 0:8].astype(BF16), x8)
            active = activate(hidden, 1, 128 * FT)
            tile = t + iota((1, 128 * FT), 1) // 128
            lanef = iota((1, 128 * FT), 1) % 128
            gone = ((tile == 0) & (lanef < 32) & (z == 0)) | ((tile == 33) & (lanef >= 96) & (z == SEG - 1))
            active = jnp.where(gone, 0.0, active)
            for h in range(FT):
                one = active[:, 128 * h : 128 * h + 128]
                hid3[t + h] = hidden[:, 128 * h : 128 * h + 128]
                act3[t + h, 0:128] = jnp.where(col2[:, 0:128] == 0, 0.0, pltpu.roll(one, 1, 1)).astype(BF16)
                act3[t + h, 128:256] = one.astype(BF16)
                act3[t + h, 256:384] = jnp.where(col2[:, 0:128] == 31, 0.0, pltpu.roll(one, 127, 1)).astype(BF16)

        def back_step(n, carry):
            i = n * STEPS
            tiles = [act3[i + e] for e in range(STEPS + 2)]
            stack = jnp.concatenate(
                [jnp.concatenate(tiles[a : a + STEPS], axis=1) for a in range(3)], axis=0
            )
            h2 = jnp.concatenate([hid3[i + 1 + e] for e in range(STEPS)], axis=1) + dot(conv_t[1], stack)
            eps = back(1, m, h2, 128 * STEPS)
            rows = x2[m, pl.ds(pl.multiple_of((i + 1) * 8, 8), 8 * STEPS), :]
            noisy = jnp.concatenate([rows[8 * e : 8 * e + 8] for e in range(STEPS)], axis=1)
            clean, prior = step_of(noisy, eps, *coefs(2, m))
            for e in range(STEPS):
                spot_at = pl.ds(pl.multiple_of((i + e) * 8, 8), 8)
                c2[0, m, spot_at, :] = clean[:, 128 * e : 128 * e + 128]
                c2[1, m, spot_at, :] = prior[:, 128 * e : 128 * e + 128]
            return carry

        lax.fori_loop(0, 32 // STEPS, back_step, 0)

    def result_to(j, slot):
        return remote(snd2.at[j], rcv2.at[slot], send2.at[j], recv2.at[slot], y, z * LANE + j)

    for j in range(LANE):
        rows = []
        for c in range(3):
            total = None
            for o in range(2):
                for m in range(2):
                    one = regroup(c2[o, m, pl.ds(128 * (j % 2) + c, 16, 8), :], j // 2, 2 * o + m)
                    total = one if total is None else jnp.where(lane1 // 32 == 2 * o + m, one, total)
            rows.append(total)
        snd2[j] = jnp.concatenate(rows, axis=0).astype(BF16)

        @pl.when((y != z) | (k != j))
        def _():
            result_to(j, k).start()

    @pl.when(y == z)
    def _():
        rcv2[k] = snd2[k]

    each_other(z, y, k, lambda j: noise_to(j, k).wait_send())
    for cond, slot, step in ((lower, LANE, 1), (upper, LANE + 1, -1)):
        @pl.when(cond)
        def _():
            for j in range(LANE):
                halo_to(j, slot, y + step).wait_send()

    each_other(z, y, k, lambda j: result_to(j, j).wait_recv())
    for j in range(LANE):
        whole = rcv2[j].astype(F32)
        for o in range(2):
            for m in range(2):
                one = regroup(whole, 2 * o + m, 0)[:, 0:32].astype(BF16)
                for c in range(3):
                    out[o, m, j, c] = one[16 * c : 16 * c + 16]
    each_other(z, y, k, lambda j: result_to(j, k).wait_send())


def shards(
    text_states, token_ids, step_ids, base_noise, upscale_noise, final_noise, t5_gain,
    base_keyval, upscale_keyval, base_input, base_time, base_gain, base_conv, base_query,
    base_output, base_head, upscale_input, upscale_time, upscale_gain, upscale_conv,
    upscale_query, upscale_output, upscale_head,
):
    early, final_states = pl.pallas_call(
        step_kernel,
        out_shape=(
            jax.ShapeDtypeStruct((2, 3, 2, 256), BF16),
            jax.ShapeDtypeStruct((2, 2, LANE, 3, 16, 32), BF16),
        ),
        in_specs=[SMEM] + [VMEM] * 10 + [ANY] * 12,
        out_specs=(VMEM, VMEM),
        scratch_shapes=[
            pltpu.VMEM((256, 4096), BF16),
            pltpu.VMEM((3, 4096, 512), BF16),
            pltpu.VMEM((512, 512), BF16),
            pltpu.VMEM((3, 1536, 512), BF16),
            pltpu.VMEM((512, 512), BF16),
            pltpu.VMEM((512, 512), BF16),
            pltpu.VMEM((2, 128, 128), BF16),
            pltpu.VMEM((2, 9, 128, 128), BF16),
            pltpu.VMEM((2, 128, 128), BF16),
            pltpu.VMEM((2, 128, 128), BF16),
            pltpu.VMEM((2, LANE, 3, 16, 32), BF16),
            pltpu.VMEM((256, 4096), BF16),
            pltpu.VMEM((256, 1536), BF16),
            pltpu.VMEM((3, 640, 1536), BF16),
            pltpu.VMEM((640, 512), F32),
            pltpu.VMEM((640, 512), BF16),
            pltpu.VMEM((640, 512), BF16),
            pltpu.VMEM((2, 8, 1024), F32),
            pltpu.VMEM((2, 8, 1024), F32),
            pltpu.VMEM((8, 128), F32),
            pltpu.VMEM((8, 128), F32),
            pltpu.VMEM((6, 128, 128), F32),
            pltpu.VMEM((2, 128, 128), BF16),
            pltpu.VMEM((2, 128, 128), BF16),
            pltpu.VMEM((2, 8, 128), BF16),
            pltpu.VMEM((2, 128, 1152), BF16),
            pltpu.VMEM((4, 256, 128), BF16),
            pltpu.VMEM((4, 144, 256), BF16),
            pltpu.VMEM((2, 1, 256), F32),
            pltpu.VMEM((2, 128, 128), F32),
            pltpu.VMEM((8, 512), F32),
            pltpu.VMEM((2, 272, 128), F32),
            pltpu.VMEM((34, 128, 128), F32),
            pltpu.VMEM((34, 384, 128), BF16),
            pltpu.VMEM((2, 2, 256, 128), F32),
            pltpu.VMEM((2, 3, 2, 256), F32),
            pltpu.VMEM((LANE, 32, 128), F32),
            pltpu.VMEM((LANE, 32, 128), BF16),
            pltpu.VMEM((LANE + 2, 32, 128), BF16),
            pltpu.VMEM((LANE, 48, 128), BF16),
            pltpu.VMEM((LANE, 48, 128), BF16),
            pltpu.SemaphoreType.DMA((14,)),
            pltpu.SemaphoreType.DMA((LANE,)),
            pltpu.SemaphoreType.DMA((LANE + 2,)),
            pltpu.SemaphoreType.DMA((LANE,)),
            pltpu.SemaphoreType.DMA((LANE,)),
            pltpu.SemaphoreType.DMA((LANE,)),
        ],
        compiler_params=pltpu.CompilerParams(
            vmem_limit_bytes=56 * 1024 * 1024, collective_id=0, has_side_effects=True
        ),
        name="denoise",
    )(
        step_ids.T, token_ids, base_noise[:, 0].transpose(1, 0, 2), upscale_noise[:, 0].transpose(1, 0, 2), t5_gain[None],
        base_input, base_gain, base_head.T, upscale_input.transpose(1, 0, 2), upscale_gain.transpose(1, 0, 2),
        upscale_head.transpose(2, 0, 1), final_noise,
        text_states.reshape(256, 4096), base_keyval, upscale_keyval, base_time, base_conv.reshape(3, 1536, 512),
        base_query, base_output, upscale_time, upscale_conv, upscale_query, upscale_output,
    )
    return early.transpose(0, 2, 1, 3)[:, :, None], final_states


def solution(mesh):
    placed = [P() for _ in range(23)]
    placed[0] = placed[3] = placed[4] = P(None, "space", None, None)
    placed[5] = P(None, None, None, "space", None)
    return jax.shard_map(
        shards,
        mesh=mesh,
        in_specs=tuple(placed),
        out_specs=(
            P(None, None, "space", None, "segment"),
            P(None, None, "segment", None, "space", None),
        ),
        check_vma=False,
    )
```

```python
import functools
import math

import jax
import jax.numpy as jnp
from jax import lax
from jax.experimental import pallas as pl
from jax.experimental.pallas import tpu as pltpu
from jax.sharding import PartitionSpec as P

MESH = pl.DeviceIdType.MESH
ANY = pl.BlockSpec(memory_space=pl.ANY)
VMEM = pl.BlockSpec(memory_space=pltpu.VMEM)
SMEM = pl.BlockSpec(memory_space=pltpu.SMEM)
F32, BF16 = jnp.float32, jnp.bfloat16
LOG2E = 1.4426950408889634
SCALE = 0.125 * LOG2E
SEG, LANE = 4, 8

STEPS = 32


def dot(a, b):
    return jnp.dot(a, b, preferred_element_type=F32)


def dot_nt(a, b):
    return lax.dot_general(a, b, (((1,), (1,)), ((), ())), preferred_element_type=F32)


def iota(shape, dim):
    return lax.broadcasted_iota(jnp.int32, shape, dim)


def place():
    z = lax.axis_index("segment")
    p = lax.axis_index("space")
    return z, p // LANE, p % LANE


def remote(src, dst, send, recv, z, p):
    return pltpu.make_async_remote_copy(
        src_ref=src, dst_ref=dst, send_sem=send, recv_sem=recv, device_id=(z, p), device_id_type=MESH
    )


def each_other(z, y, k, body):
    for j in range(LANE):
        @pl.when((y != z) | (k != j))
        def _():
            body(j)


def step_kernel(
    steps, ids, bx, ux, t5g, b_in, b_gain, b_head, u_in, u_gain, u_head,
    noise_h, text_h, bkv_h, ukv_h, btime_h, bconv_h, bq_h, bo_h, utime_h, uconv_h, uq_h, uo_h,
    early, rcv2,
    text_v, kv_w, btime_v, bconv_v, bq_v, bo_v, utime_v, uconv_v, uq_v, uo_v, noise_v,
    ctx, kv, taps, hid, query, att, x8b, x8u, rows8, aug8, gcol, wq_t, wo_t, wh_t, conv_t,
    kcat, vcat, mask_row, mask_col, head8, x2, hid3, act3, c2, early_v,
    snd, snd_b, rcv, snd2, sems, send, recv, halo_send, send2, recv2,
):
    z, y, k = place()
    p = y * LANE + k

    barrier = pltpu.get_barrier_semaphore()

    def hello(z_to, p_to):
        pl.semaphore_signal(barrier, inc=1, device_id=(z_to, p_to), device_id_type=MESH)

    each_other(z, y, k, lambda j: hello(y, z * LANE + j))

    @pl.when(z > 0)
    def _():
        hello(y, z * LANE - 1)

    @pl.when(z < SEG - 1)
    def _():
        hello(y, z * LANE + LANE)

    copies = [
        pltpu.make_async_copy(src, dst, sems.at[n])
        for n, (src, dst) in enumerate(
            [
                (noise_h.at[:, pl.ds(z * LANE, LANE)], noise_v),
                (utime_h, utime_v), (uq_h, uq_v), (uo_h, uo_v), (uconv_h, uconv_v), (btime_h, btime_v),
                (text_h, text_v), (bconv_h, bconv_v),
            ]
            + [(bkv_h.at[:, 512 * n : 512 * n + 512], kv_w.at[n]) for n in range(2)]
            + [(ukv_h.at[n], kv_w.at[2, :, 256 * n : 256 * n + 256]) for n in range(2)]
            + [(bq_h, bq_v), (bo_h, bo_v)]
        )
    ]
    for copy in copies:
        copy.start()
    at = dict(noise=0, utime=1, uq=2, uo=3, uconv=4, btime=5, text=6, bconv=7, kv=8, bq=12, bo=13)

    copies[at["noise"]].wait()
    packed = jnp.zeros((LANE * 24, 128), F32)
    for m in range(2):
        rows = noise_v[m].astype(F32)
        for half in range(2):
            group = 2 * m + half
            place_at = (iota((32, 128), 0) + 32 * group == iota((32, 128), 1)).astype(F32).astype(BF16)
            packed += dot(rows[:, :, 8 * half : 8 * half + 8, :].reshape(LANE * 24, 32).astype(BF16), place_at)
    snd[:, 0:24, :] = packed.reshape(LANE, 24, 128)
    snd[:, 24:32, :] = jnp.zeros((LANE, 8, 128), F32)
    snd_b[...] = snd[...].astype(BF16)

    lower = (k == LANE - 1) & (y < SEG - 1)
    upper = (k == 0) & (y > 0)
    extra = jnp.where(lower | upper, LANE, 0)
    pl.semaphore_wait(barrier, LANE - 1 + jnp.where(y != z, 1, 0) + extra)

    def noise_to(j, slot):
        return remote(snd_b.at[j], rcv.at[slot], send.at[j], recv.at[slot], y, z * LANE + j)

    def halo_to(j, slot, to):
        return remote(snd_b.at[j], rcv.at[slot], halo_send.at[j], recv.at[slot], to, z * LANE + j)

    each_other(z, y, k, lambda j: noise_to(j, k).start())
    for cond, slot, step in ((lower, LANE, 1), (upper, LANE + 1, -1)):
        @pl.when(cond)
        def _():
            for j in range(LANE):
                halo_to(j, slot, y + step).start()

    @pl.when(y == z)
    def _():
        rcv[k] = snd_b[k]

    lane128 = iota((128, 128), 1)
    sub128 = iota((128, 128), 0)
    for m in range(2):
        x8b[m] = jnp.zeros((8, 1024), F32)
        x8u[m] = jnp.zeros((8, 1024), F32)
        for c in range(3):
            x8b[m, c : c + 1, :] = bx[c].astype(F32)[m : m + 1]
            x8u[m, c : c + 1, :] = ux[c].astype(F32)[m : m + 1]
        row = jnp.where(ids[m, pl.ds(p, 1), :] != 0, 0.0, -1e30)
        mask_row[m, :, 0:128] = row
        mask_row[m, :, 128:256] = row
        rows8[...] = jnp.broadcast_to(row, (8, 128))
        column = jnp.transpose(rows8[...])[:, 0:1]
        mask_col[m] = jnp.broadcast_to(column, (128, 128))
    head8[...] = jnp.zeros_like(head8)
    head8[0:3, :] = b_head[...].astype(F32)

    def code(width, first):
        row, lane = iota((8, width), 0), iota((8, width), 1)
        step = jnp.zeros((8, width), F32)
        for s in range(2):
            for m in range(2):
                section = min(first + s, 2)
                step = jnp.where(row == 2 * s + m, steps[m, section].astype(F32), step)
        half = width // 2
        angle = step * jnp.exp((-math.log(10000.0) / half) * (lane % half).astype(F32))
        return jnp.where(lane < half, jnp.sin(angle), jnp.cos(angle)).astype(BF16)

    def coefs(s, m):
        step = jnp.full((8, 128), steps[m, s].astype(F32))

        def alpha(at_step):
            return jnp.cos((at_step / 1000.0 + 0.008) * (math.pi / 2 / 1.008)) ** 2

        level, earlier = alpha(step), alpha(step - 50.0)
        return jnp.sqrt(1.0 - level), 1.0 / jnp.sqrt(level), jnp.sqrt(earlier), jnp.sqrt(1.0 - earlier)

    for n in range(1, 5):
        copies[n].wait()
    code_up = code(128, 1)
    code_base = code(512, 0)
    for s in range(2):
        emb = dot(code_up, utime_v[s])
        for m in range(2):
            for c in range(6):
                aug8[c : c + 1, :] = u_in[c].astype(F32)[s : s + 1]
            one = emb[2 * s + m : 2 * s + m + 1, :]
            high = one.astype(BF16).astype(F32)
            aug8[6:7, :] = high
            aug8[7:8, :] = one - high
            x8 = jnp.transpose(aug8[...]).astype(BF16)
            gcol[2 + 2 * s + m, :, 0:8] = x8.astype(F32)
        rows8[...] = jnp.zeros((8, 128), F32)
        for c in range(3):
            rows8[c : c + 1, :] = u_gain[c, s : s + 1, :]
        turned = jnp.transpose(rows8[...])
        gcol[s] = jnp.broadcast_to(turned[:, 0:1] * 0.5, (128, 128))
        wq_t[s] = jnp.transpose(uq_v[s].astype(F32) * (turned[:, 1:2] * SCALE)).astype(BF16)
        wo_t[s] = jnp.transpose(uo_v[s].astype(F32)).astype(BF16)
        rows8[...] = jnp.zeros((8, 128), F32)
        for c in range(3):
            rows8[c : c + 1, :] = u_head[c].astype(F32)[s : s + 1] * u_gain[2, s : s + 1, :]
        wh_t[s] = rows8[...].astype(BF16)
        for tap in range(9):
            conv_t[s, :, 128 * tap : 128 * tap + 128] = jnp.transpose(uconv_v[s, tap].astype(F32)).astype(BF16)

    copies[at["btime"]].wait()
    emb_b = dot(code_base, btime_v[...])
    w_in = b_in[...]
    for m in range(2):
        rolled = pltpu.roll(x8b[m], jnp.mod(32 - 256 * z, 1024), 1)
        own_t = jnp.transpose(rolled[:, 0:384])[0:320, :]
        blk_t = jnp.transpose(x8b[m, :, 0:384])[0:288, :].reshape(9, 32, 8)[:, 0:16, :].reshape(144, 8)
        pix = jnp.concatenate([own_t, blk_t], axis=0)[:, 0:3].astype(BF16)
        hidden = dot(pix, w_in) + emb_b[m : m + 1, :]
        scale = lax.rsqrt(jnp.mean(hidden * hidden, axis=-1, keepdims=True) + 1e-6)
        half = hidden * scale * (b_gain[0:1, :] * 0.5)
        active = half + half * jnp.tanh(half)
        hid[256 * m : 256 * m + 256, :] = hidden[32:288]
        hid[512 + 64 * m : 576 + 64 * m, :] = hidden[320:464].reshape(9, 16, 512)[0:8, 0:8].reshape(64, 512)
        own = active[0:320]
        line = iota((320, 1), 0)
        gone = ((line < 32) & (z == 0)) | ((line >= 288) & (z == SEG - 1))
        own = jnp.where(gone, 0.0, own)
        blk = active[320:464]
        col = line % 32
        bcol = iota((144, 1), 0) % 16
        for b in range(3):
            if b == 0:
                mine = jnp.where(col == 0, 0.0, pltpu.roll(own, 1, 0))
                near = jnp.where(bcol == 0, 0.0, pltpu.roll(blk, 1, 0))
            elif b == 1:
                mine, near = own, blk
            else:
                mine = jnp.where(col == 31, 0.0, pltpu.roll(own, 319, 0))
                near = pltpu.roll(blk, 143, 0)
            mine = mine.astype(BF16)
            near = near.reshape(9, 16, 512)[:, 0:8].reshape(72, 512)
            near = jnp.concatenate([jnp.zeros((8, 512), F32), near], axis=0)
            for a in range(3):
                taps[256 * m : 256 * m + 256, 512 * (3 * a + b) : 512 * (3 * a + b) + 512] = mine[32 * a : 32 * a + 256]
                taps[512 + 64 * m : 576 + 64 * m, 512 * (3 * a + b) : 512 * (3 * a + b) + 512] = near[8 * a : 8 * a + 64].astype(BF16)

    copies[at["text"]].wait()

    def norm_step(i, carry):
        at_row = pl.multiple_of(i * 64, 64)
        states = text_v[pl.ds(at_row, 64), :].astype(F32)
        scale = lax.rsqrt(jnp.mean(states * states, axis=-1, keepdims=True) + 1e-6)
        ctx[pl.ds(at_row, 64), :] = (states * scale * t5g[...]).astype(BF16)
        return carry

    lax.fori_loop(0, 4, norm_step, 0)
    copies[at["bconv"]].wait()

    hid[...] += dot(taps[...], bconv_v[...])

    for n in range(3):
        copies[at["kv"] + n].wait()
        if n == 2:
            copies[at["kv"] + 3].wait()
        kv[:, 512 * n : 512 * n + 512] = dot(ctx[...], kv_w[n]).astype(BF16)

    for s in range(2):
        for m in range(2):
            key = kv[128 * m : 128 * m + 128, 1024 + 256 * s : 1152 + 256 * s]
            val = jnp.transpose(kv[128 * m : 128 * m + 128, 1152 + 256 * s : 1280 + 256 * s].astype(F32)).astype(BF16)
            zero = jnp.zeros_like(key)
            kcat[2 * s + m, 0:128, :] = jnp.where(lane128 < 64, key, zero)
            kcat[2 * s + m, 128:256, :] = jnp.where(lane128 < 64, zero, key)
            vcat[2 * s + m, 0:128, 0:128] = jnp.where(sub128 < 64, val, zero)
            vcat[2 * s + m, 0:128, 128:256] = jnp.where(sub128 < 64, zero, val)
            head_of = iota((16, 256), 1) // 128
            vcat[2 * s + m, 128:144, :] = (head_of == iota((16, 256), 0)).astype(F32).astype(BF16)

    copies[at["bq"]].wait()
    copies[at["bo"]].wait()
    h2 = hid[...]
    scale = lax.rsqrt(jnp.mean(h2 * h2, axis=-1, keepdims=True) + 1e-6)
    query[...] = (dot((h2 * scale * b_gain[1:2, :]).astype(BF16), bq_v[...]) * SCALE).astype(BF16)
    for m in range(2):
        for pair in range(4):
            lo = 128 * pair
            key = kv[128 * m : 128 * m + 128, lo : lo + 128]
            val = kv[128 * m : 128 * m + 128, 512 + lo : 640 + lo]
            zero = jnp.zeros_like(key)
            keys = jnp.concatenate([jnp.where(lane128 < 64, key, zero), jnp.where(lane128 < 64, zero, key)], axis=0)
            vals = jnp.concatenate([jnp.where(lane128 < 64, val, zero), jnp.where(lane128 < 64, zero, val)], axis=0)
            ones = ((iota((256, 128), 0) < 128) == (iota((256, 128), 1) < 64)).astype(F32).astype(BF16)
            vals = jnp.concatenate([vals, ones], axis=1)
            q = jnp.concatenate(
                [query[256 * m : 256 * m + 256, lo : lo + 128], query[512 + 64 * m : 576 + 64 * m, lo : lo + 128]], axis=0
            )
            score = dot_nt(q, keys) + mask_row[m]
            left, right = score[:, 0:128], score[:, 128:256]
            left = jnp.exp2(left - jnp.max(left, axis=-1, keepdims=True))
            right = jnp.exp2(right - jnp.max(right, axis=-1, keepdims=True))
            mixed = dot(jnp.concatenate([left, right], axis=1).astype(BF16), vals)
            mixed = (mixed[:, 0:128] / mixed[:, 128:256]).astype(BF16)
            att[256 * m : 256 * m + 256, lo : lo + 128] = mixed[0:256]
            att[512 + 64 * m : 576 + 64 * m, lo : lo + 128] = mixed[256:320]
    h3 = hid[...] + dot(att[...], bo_v[...])
    scale = lax.rsqrt(jnp.mean(h3 * h3, axis=-1, keepdims=True) + 1e-6)
    eps = dot_nt(head8[...].astype(BF16), (h3 * scale * b_gain[2:3, :]).astype(BF16))

    def step_of(noisy, eps, c0, c1, c2_, c3):
        c0, c1, c2_, c3 = (jnp.concatenate([c] * (eps.shape[1] // 128), axis=1) for c in (c0, c1, c2_, c3))
        clean = jnp.clip((noisy - c0 * eps) * c1, -1.0, 1.0)
        return clean, c2_ * clean + c3 * eps

    pick_k, pick_l = iota((256, 128), 0), iota((256, 128), 1)
    noisy = jnp.zeros((8, 128), F32)
    for m in range(2):
        whole = pltpu.roll(x8b[m], jnp.mod(0 - 256 * z, 1024), 1)[:, 0:256]
        _, prior = step_of(whole, eps[:, 256 * m : 256 * m + 256], *coefs(0, m))
        for c in range(3):
            early_v[0, c, m : m + 1, :] = prior[c : c + 1]
        spot = pick_l - 64 * m
        sel = (spot >= 0) & (spot < 64) & ((pick_k >> 5) == (spot >> 3)) & ((pick_k & 31) == (spot & 7))
        noisy += dot(x8b[m, :, 0:256].astype(BF16), sel.astype(F32).astype(BF16))
    first_half = iota((8, 128), 1) < 64
    mixed_coefs = tuple(jnp.where(first_half, a, b) for a, b in zip(coefs(0, 0), coefs(0, 1)))
    region, _ = step_of(noisy, eps[:, 512:640], *mixed_coefs)
    region = region.astype(BF16)

    def back(s, ms, h2, width):
        scale = lax.rsqrt(jnp.sum(h2 * h2, axis=0, keepdims=True) * (1.0 / 128.0) + 1e-6)
        q = (dot(wq_t[s], h2.astype(BF16)) * scale).astype(BF16)
        both = []
        for n, m in enumerate(ms):
            score = dot(kcat[2 * s + m], q[:, width * n : width * n + width])
            mask = jnp.concatenate([mask_col[m]] * (width // 128), axis=1)
            left, right = score[0:128] + mask, score[128:256] + mask
            left = jnp.exp2(left - jnp.max(left, axis=0, keepdims=True)).astype(BF16)
            right = jnp.exp2(right - jnp.max(right, axis=0, keepdims=True)).astype(BF16)
            mixed = dot(vcat[2 * s + m], jnp.concatenate([left, right], axis=0))
            top = mixed[0:64] * (1.0 / mixed[128:129])
            bottom = mixed[64:128] * (1.0 / mixed[129:130])
            both.append(jnp.concatenate([top, bottom], axis=0).astype(BF16))
        both = both[0] if len(both) == 1 else jnp.concatenate(both, axis=1)
        h3 = h2 + dot(wo_t[s], both)
        scale = lax.rsqrt(jnp.sum(h3 * h3, axis=0, keepdims=True) * (1.0 / 128.0) + 1e-6)
        return dot(wh_t[s], h3.astype(BF16)) * scale

    def activate(hidden, s, width):
        scale = lax.rsqrt(jnp.sum(hidden * hidden, axis=0, keepdims=True) * (1.0 / 128.0) + 1e-6)
        gain = jnp.concatenate([gcol[s]] * (width // 128), axis=1)
        half = hidden * scale * gain
        return half + half * jnp.tanh(half)

    lane1 = iota((1, 128), 1)

    def regroup(value, source, target):
        by = 32 * (target - source) % 128
        return pltpu.roll(value, by, 1) if by else value

    lanes = iota((1, 768), 1)
    lanes = jnp.where(lanes >= 384, lanes - 384, lanes)
    row_of = 8 * z - 2 + (lanes >> 5)
    col_of = lanes & 31
    inside = (row_of >= 0) & (row_of < 32)
    spread_k = iota((128, 384), 0)
    spread_l = iota((128, 384), 1)
    spread_at = (((8 * z + 2 + (spread_l >> 5)) >> 2) - 1) * 8 + ((spread_l & 31) >> 2)
    spread_at = jnp.where((spread_at >= 0) & (spread_at < 64), spread_at, -1000)
    which = iota((8, 384), 0)
    noisy, hidden = [], []
    for m in range(2):
        x = pltpu.roll(x8u[m], jnp.mod(64 - 256 * z, 1024), 1)[:, 0:384]
        cond = pltpu.roll(dot(region, (spread_k == spread_at + 64 * m).astype(F32).astype(BF16)), 3, 0)
        x8 = jnp.where(which < 3, x, jnp.where(which < 6, cond, 1.0))
        hidden.append(dot(gcol[2 + m, :, 0:8].astype(BF16), x8.astype(BF16)))
        noisy.append(x)
    hidden = jnp.concatenate(hidden, axis=1)
    active = jnp.where(inside, activate(hidden, 0, 768), 0.0)
    stack = [
        jnp.where(col_of == 0, 0.0, pltpu.roll(active, 1, 1)),
        active,
        jnp.where(col_of == 31, 0.0, pltpu.roll(active, 767, 1)),
    ]
    stack = [pltpu.roll(one, 32, 1) for one in stack] + stack + [pltpu.roll(one, 736, 1) for one in stack]
    stack = jnp.concatenate([one.astype(BF16) for one in stack], axis=0)
    eps = back(0, (0, 1), hidden + dot(conv_t[0], stack), 384)
    for m in range(2):
        clean, prior = step_of(noisy[m], eps[:, 384 * m : 384 * m + 384], *coefs(1, m))
        prior = pltpu.roll(prior, 320, 1)[:, 0:256]
        for c in range(3):
            early_v[1, c, m : m + 1, :] = prior[c : c + 1]
        clean = clean.astype(BF16).astype(F32)

        def rows_at(first):
            total = None
            for g in range(4):
                row = first + 2 * g
                one = regroup(clean[:, 128 * (row // 4) : 128 * (row // 4) + 128], row % 4, g)
                total = one if total is None else jnp.where((lane1 >> 5) == g, one, total)
            return total

        x2[m] = jnp.ones((34 * 8, 128), F32)
        even, odd = rows_at(2), rows_at(3)
        above, below = rows_at(1), rows_at(4)
        for c in range(3):
            x2[m, pl.ds(8 + 3 + c, 16, 8), :] = jnp.broadcast_to(even[c : c + 1], (16, 128))
            x2[m, pl.ds(8 * 17 + 3 + c, 16, 8), :] = jnp.broadcast_to(odd[c : c + 1], (16, 128))
            x2[m, 3 + c : 4 + c, :] = above[c : c + 1]
            x2[m, 33 * 8 + 3 + c : 33 * 8 + 4 + c, :] = below[c : c + 1]

    early[...] = early_v[...].astype(BF16)
    each_other(z, y, k, lambda j: noise_to(j, j).wait_recv())

    @pl.when(z > 0)
    def _():
        noise_to(0, LANE).wait_recv()

    @pl.when(z < SEG - 1)
    def _():
        noise_to(0, LANE + 1).wait_recv()

    @pl.when(z == 0)
    def _():
        rcv[LANE] = jnp.zeros((32, 128), BF16)

    @pl.when(z == SEG - 1)
    def _():
        rcv[LANE + 1] = jnp.zeros((32, 128), BF16)

    blocks = [rcv[n].astype(F32)[0:24] for n in range(LANE + 2)]
    for m in range(2):
        edge = {}
        for h in range(2):
            for half in range(2):
                group = 2 * m + half
                total = regroup(blocks[h], group, 0)
                for g in range(1, 4):
                    total = jnp.where((lane1 >> 5) == g, regroup(blocks[2 * g + h], group, g), total)
                edge[h, half] = total
                for c in range(3):
                    x2[m, pl.ds(8 * (1 + 16 * h + 8 * half) + c, 8, 8), :] = total[8 * c : 8 * c + 8]
        top = regroup(blocks[LANE], 2 * m + 1, 0)
        low = regroup(blocks[LANE + 1], 2 * m, 3)
        over = pltpu.roll(edge[1, 1], 32, 1)
        under = pltpu.roll(edge[0, 0], 96, 1)
        for c in range(3):
            x2[m, c : c + 1, :] = jnp.where(lane1 < 32, top, over)[8 * c + 7 : 8 * c + 8]
            x2[m, 33 * 8 + c : 33 * 8 + c + 1, :] = jnp.where(lane1 >= 96, low, under)[8 * c : 8 * c + 1]

    def result_to(m, j, slot):
        return remote(snd2.at[m, j], rcv2.at[m, slot], send2.at[m, j], recv2.at[m, slot], y, z * LANE + j)

    FT = 17
    lanef = iota((1, 128 * FT), 1)
    colf = iota((1, 128), 1) & 31
    for m in range(2):
        for n in range(34 // FT):
            t = n * FT
            rows = x2[m, t * 8 : (t + FT) * 8, :]
            x8 = jnp.concatenate([rows[8 * e : 8 * e + 8] for e in range(FT)], axis=1).astype(BF16)
            hidden = dot(gcol[4 + m, :, 0:8].astype(BF16), x8)
            active = activate(hidden, 1, 128 * FT)
            if n == 0:
                active = jnp.where((lanef < 32) & (z == 0), 0.0, active)
            else:
                active = jnp.where((lanef >= 128 * FT - 32) & (z == SEG - 1), 0.0, active)
            for h in range(FT):
                one = active[:, 128 * h : 128 * h + 128]
                hid3[m, t + h] = hidden[:, 128 * h : 128 * h + 128]
                act3[m, t + h, 0:128] = jnp.where(colf == 0, 0.0, pltpu.roll(one, 1, 1)).astype(BF16)
                act3[m, t + h, 128:256] = one.astype(BF16)
                act3[m, t + h, 256:384] = jnp.where(colf == 31, 0.0, pltpu.roll(one, 127, 1)).astype(BF16)

        for i in range(0, 32, STEPS):
            tiles = [act3[m, i + e] for e in range(STEPS + 2)]
            stack = jnp.concatenate(
                [jnp.concatenate(tiles[a : a + STEPS], axis=1) for a in range(3)], axis=0
            )
            h2 = jnp.concatenate([hid3[m, i + 1 + e] for e in range(STEPS)], axis=1) + dot(conv_t[1], stack)
            eps = back(1, (m,), h2, 128 * STEPS)
            rows = x2[m, (i + 1) * 8 : (i + 1 + STEPS) * 8, :]
            noisy = jnp.concatenate([rows[8 * e : 8 * e + 8] for e in range(STEPS)], axis=1)
            clean, prior = step_of(noisy, eps, *coefs(2, m))
            for e in range(STEPS):
                c2[0, m, (i + e) * 8 : (i + e) * 8 + 8, :] = clean[:, 128 * e : 128 * e + 128]
                c2[1, m, (i + e) * 8 : (i + e) * 8 + 8, :] = prior[:, 128 * e : 128 * e + 128]

        for j in range(LANE):
            rows = []
            for c in range(3):
                total = None
                for o in range(2):
                    for half in range(2):
                        one = c2[o, m, pl.ds(128 * (j % 2) + 64 * half + c, 8, 8), :]
                        one = regroup(one, j // 2, 2 * o + half)
                        total = one if total is None else jnp.where((lane1 >> 5) == 2 * o + half, one, total)
                rows.append(total)
            rows.append(jnp.zeros((8, 128), F32))
            snd2[m, j] = jnp.concatenate(rows, axis=0).astype(BF16)

        each_other(z, y, k, lambda j: result_to(m, j, k).start())

        @pl.when(y == z)
        def _():
            rcv2[m, k] = snd2[m, k]

    each_other(z, y, k, lambda j: noise_to(j, k).wait_send())
    for cond, slot, step in ((lower, LANE, 1), (upper, LANE + 1, -1)):
        @pl.when(cond)
        def _():
            for j in range(LANE):
                halo_to(j, slot, y + step).wait_send()

    for m in range(2):
        each_other(z, y, k, lambda j: result_to(m, j, j).wait_recv())
    for m in range(2):
        each_other(z, y, k, lambda j: result_to(m, j, k).wait_send())


def unpack_kernel(early_in, got, early, out):
    early[...] = early_in[...]
    for m in range(2):
        for j in range(LANE):
            whole = got[m, j].astype(F32)[0:24]
            for o in range(2):
                upper, lower = (
                    pltpu.roll(whole, (128 - 32 * (2 * o + half)) % 128, 1)[:, 0:32] if 2 * o + half else whole[:, 0:32]
                    for half in range(2)
                )
                for c in range(3):
                    both = jnp.concatenate([upper[8 * c : 8 * c + 8], lower[8 * c : 8 * c + 8]], axis=0)
                    out[o, m, j, c] = both.astype(BF16)


def shards(
    text_states, token_ids, step_ids, base_noise, upscale_noise, final_noise, t5_gain,
    base_keyval, upscale_keyval, base_input, base_time, base_gain, base_conv, base_query,
    base_output, base_head, upscale_input, upscale_time, upscale_gain, upscale_conv,
    upscale_query, upscale_output, upscale_head,
):
    early, got = pl.pallas_call(
        step_kernel,
        out_shape=(
            jax.ShapeDtypeStruct((2, 3, 2, 256), BF16),
            jax.ShapeDtypeStruct((2, LANE, 32, 128), BF16),
        ),
        in_specs=[SMEM] + [VMEM] * 10 + [ANY] * 12,
        out_specs=(VMEM, VMEM),
        scratch_shapes=[
            pltpu.VMEM((256, 4096), BF16),
            pltpu.VMEM((3, 4096, 512), BF16),
            pltpu.VMEM((512, 512), BF16),
            pltpu.VMEM((4608, 512), BF16),
            pltpu.VMEM((512, 512), BF16),
            pltpu.VMEM((512, 512), BF16),
            pltpu.VMEM((2, 128, 128), BF16),
            pltpu.VMEM((2, 9, 128, 128), BF16),
            pltpu.VMEM((2, 128, 128), BF16),
            pltpu.VMEM((2, 128, 128), BF16),
            pltpu.VMEM((2, LANE, 3, 16, 32), BF16),
            pltpu.VMEM((256, 4096), BF16),
            pltpu.VMEM((256, 1536), BF16),
            pltpu.VMEM((640, 4608), BF16),
            pltpu.VMEM((640, 512), F32),
            pltpu.VMEM((640, 512), BF16),
            pltpu.VMEM((640, 512), BF16),
            pltpu.VMEM((2, 8, 1024), F32),
            pltpu.VMEM((2, 8, 1024), F32),
            pltpu.VMEM((8, 128), F32),
            pltpu.VMEM((8, 128), F32),
            pltpu.VMEM((6, 128, 128), F32),
            pltpu.VMEM((2, 128, 128), BF16),
            pltpu.VMEM((2, 128, 128), BF16),
            pltpu.VMEM((2, 8, 128), BF16),
            pltpu.VMEM((2, 128, 1152), BF16),
            pltpu.VMEM((4, 256, 128), BF16),
            pltpu.VMEM((4, 144, 256), BF16),
            pltpu.VMEM((2, 1, 256), F32),
            pltpu.VMEM((2, 128, 128), F32),
            pltpu.VMEM((8, 512), F32),
            pltpu.VMEM((2, 272, 128), F32),
            pltpu.VMEM((2, 34, 128, 128), F32),
            pltpu.VMEM((2, 34, 384, 128), BF16),
            pltpu.VMEM((2, 2, 256, 128), F32),
            pltpu.VMEM((2, 3, 2, 256), F32),
            pltpu.VMEM((LANE, 32, 128), F32),
            pltpu.VMEM((LANE, 32, 128), BF16),
            pltpu.VMEM((LANE + 2, 32, 128), BF16),
            pltpu.VMEM((2, LANE, 32, 128), BF16),
            pltpu.SemaphoreType.DMA((14,)),
            pltpu.SemaphoreType.DMA((LANE,)),
            pltpu.SemaphoreType.DMA((LANE + 2,)),
            pltpu.SemaphoreType.DMA((LANE,)),
            pltpu.SemaphoreType.DMA((2, LANE)),
            pltpu.SemaphoreType.DMA((2, LANE)),
        ],
        compiler_params=pltpu.CompilerParams(
            vmem_limit_bytes=56 * 1024 * 1024, collective_id=0, has_side_effects=True
        ),
        name="denoise",
    )(
        step_ids.T, token_ids, base_noise[:, 0].transpose(1, 0, 2), upscale_noise[:, 0].transpose(1, 0, 2), t5_gain[None],
        base_input, base_gain, base_head.T, upscale_input.transpose(1, 0, 2), upscale_gain.transpose(1, 0, 2),
        upscale_head.transpose(2, 0, 1), final_noise,
        text_states.reshape(256, 4096), base_keyval, upscale_keyval, base_time, base_conv.reshape(4608, 512),
        base_query, base_output, upscale_time, upscale_conv, upscale_query, upscale_output,
    )
    early, final_states = pl.pallas_call(
        unpack_kernel,
        out_shape=(
            jax.ShapeDtypeStruct((2, 3, 2, 256), BF16),
            jax.ShapeDtypeStruct((2, 2, LANE, 3, 16, 32), BF16),
        ),
        in_specs=[VMEM] * 2,
        out_specs=(VMEM, VMEM),
        compiler_params=pltpu.CompilerParams(vmem_limit_bytes=8 * 1024 * 1024),
        name="unpack",
    )(early, got)
    return early.transpose(0, 2, 1, 3)[:, :, None], final_states


def solution(mesh):
    placed = [P() for _ in range(23)]
    placed[0] = placed[3] = placed[4] = P(None, "space", None, None)
    placed[5] = P(None, None, None, "space", None)
    return jax.shard_map(
        shards,
        mesh=mesh,
        in_specs=tuple(placed),
        out_specs=(
            P(None, None, "space", None, "segment"),
            P(None, None, "segment", None, "space", None),
        ),
        check_vma=False,
    )
```

```python
import functools
import math

import jax
import jax.numpy as jnp
from jax import lax
from jax.experimental import pallas as pl
from jax.experimental.pallas import tpu as pltpu
from jax.sharding import PartitionSpec as P

MESH = pl.DeviceIdType.MESH
ANY = pl.BlockSpec(memory_space=pl.ANY)
VMEM = pl.BlockSpec(memory_space=pltpu.VMEM)
SMEM = pl.BlockSpec(memory_space=pltpu.SMEM)
F32, BF16 = jnp.float32, jnp.bfloat16
LOG2E = 1.4426950408889634
SCALE = 0.125 * LOG2E
SEG, LANE = 4, 8

STEPS = 32


def dot(a, b):
    return jnp.dot(a, b, preferred_element_type=F32)


def dot_nt(a, b):
    return lax.dot_general(a, b, (((1,), (1,)), ((), ())), preferred_element_type=F32)


def iota(shape, dim):
    return lax.broadcasted_iota(jnp.int32, shape, dim)


def place():
    z = lax.axis_index("segment")
    p = lax.axis_index("space")
    return z, p // LANE, p % LANE


def remote(src, dst, send, recv, z, p):
    return pltpu.make_async_remote_copy(
        src_ref=src, dst_ref=dst, send_sem=send, recv_sem=recv, device_id=(z, p), device_id_type=MESH
    )


def each_other(z, y, k, body):
    for j in range(LANE):
        @pl.when((y != z) | (k != j))
        def _():
            body(j)


def step_kernel(
    steps, ids, bx, ux, t5g, b_in, b_gain, b_head, u_in, u_gain, u_head,
    noise_h, text_h, bkv_h, ukv_h, btime_h, bconv_h, bq_h, bo_h, utime_h, uconv_h, uq_h, uo_h,
    early, rcv2,
    text_v, kv_w, btime_v, bconv_v, bq_v, bo_v, utime_v, uconv_v, uq_v, uo_v, noise_v,
    ctx, kv, taps, hid, query, att, x8b, x8u, rows8, aug8, gcol, wq_t, wo_t, wh_t, conv_t,
    kcat, vcat, mask_row, mask_col, head8, x2, hid3, act3, c2, early_v,
    snd, snd_b, rcv, snd2, sems, send, recv, halo_send, send2, recv2,
):
    z, y, k = place()
    p = y * LANE + k

    barrier = pltpu.get_barrier_semaphore()

    def hello(z_to, p_to):
        pl.semaphore_signal(barrier, inc=1, device_id=(z_to, p_to), device_id_type=MESH)

    each_other(z, y, k, lambda j: hello(y, z * LANE + j))

    @pl.when(z > 0)
    def _():
        hello(y, z * LANE - 1)

    @pl.when(z < SEG - 1)
    def _():
        hello(y, z * LANE + LANE)

    copies = [
        pltpu.make_async_copy(src, dst, sems.at[n])
        for n, (src, dst) in enumerate(
            [
                (utime_h, utime_v), (uq_h, uq_v), (uo_h, uo_v), (uconv_h, uconv_v), (btime_h, btime_v),
                (text_h, text_v), (noise_h.at[:, pl.ds(z * LANE, LANE)], noise_v), (bconv_h, bconv_v),
            ]
            + [(bkv_h.at[:, 512 * n : 512 * n + 512], kv_w.at[n]) for n in range(2)]
            + [(ukv_h.at[n], kv_w.at[2, :, 256 * n : 256 * n + 256]) for n in range(2)]
            + [(bq_h, bq_v), (bo_h, bo_v)]
        )
    ]
    for copy in copies:
        copy.start()
    at = dict(utime=0, uq=1, uo=2, uconv=3, btime=4, text=5, noise=6, bconv=7, kv=8, bq=12, bo=13)

    lane128 = iota((128, 128), 1)
    sub128 = iota((128, 128), 0)
    for m in range(2):
        x8b[m] = jnp.zeros((8, 1024), F32)
        x8u[m] = jnp.zeros((8, 1024), F32)
        for c in range(3):
            x8b[m, c : c + 1, :] = bx[c].astype(F32)[m : m + 1]
            x8u[m, c : c + 1, :] = ux[c].astype(F32)[m : m + 1]
        row = jnp.where(ids[m, pl.ds(p, 1), :] != 0, 0.0, -1e30)
        mask_row[m, :, 0:128] = row
        mask_row[m, :, 128:256] = row
        rows8[...] = jnp.broadcast_to(row, (8, 128))
        column = jnp.transpose(rows8[...])[:, 0:1]
        mask_col[m] = jnp.broadcast_to(column, (128, 128))
    head8[...] = jnp.zeros_like(head8)
    head8[0:3, :] = b_head[...].astype(F32)

    def code(width, first):
        row, lane = iota((8, width), 0), iota((8, width), 1)
        step = jnp.zeros((8, width), F32)
        for s in range(2):
            for m in range(2):
                section = min(first + s, 2)
                step = jnp.where(row == 2 * s + m, steps[m, section].astype(F32), step)
        half = width // 2
        angle = step * jnp.exp((-math.log(10000.0) / half) * (lane % half).astype(F32))
        return jnp.where(lane < half, jnp.sin(angle), jnp.cos(angle)).astype(BF16)

    def coefs(s, m):
        step = jnp.full((8, 128), steps[m, s].astype(F32))

        def alpha(at_step):
            return jnp.cos((at_step / 1000.0 + 0.008) * (math.pi / 2 / 1.008)) ** 2

        level, earlier = alpha(step), alpha(step - 50.0)
        return jnp.sqrt(1.0 - level), 1.0 / jnp.sqrt(level), jnp.sqrt(earlier), jnp.sqrt(1.0 - earlier)

    for n in range(4):
        copies[n].wait()
    code_up = code(128, 1)
    code_base = code(512, 0)
    for s in range(2):
        emb = dot(code_up, utime_v[s])
        for m in range(2):
            for c in range(6):
                aug8[c : c + 1, :] = u_in[c].astype(F32)[s : s + 1]
            one = emb[2 * s + m : 2 * s + m + 1, :]
            high = one.astype(BF16).astype(F32)
            aug8[6:7, :] = high
            aug8[7:8, :] = one - high
            x8 = jnp.transpose(aug8[...]).astype(BF16)
            gcol[2 + 2 * s + m, :, 0:8] = x8.astype(F32)
        rows8[...] = jnp.zeros((8, 128), F32)
        for c in range(3):
            rows8[c : c + 1, :] = u_gain[c, s : s + 1, :]
        turned = jnp.transpose(rows8[...])
        gcol[s] = jnp.broadcast_to(turned[:, 0:1] * 0.5, (128, 128))
        wq_t[s] = jnp.transpose(uq_v[s].astype(F32) * (turned[:, 1:2] * SCALE)).astype(BF16)
        wo_t[s] = jnp.transpose(uo_v[s].astype(F32)).astype(BF16)
        rows8[...] = jnp.zeros((8, 128), F32)
        for c in range(3):
            rows8[c : c + 1, :] = u_head[c].astype(F32)[s : s + 1] * u_gain[2, s : s + 1, :]
        wh_t[s] = rows8[...].astype(BF16)
        for tap in range(9):
            conv_t[s, :, 128 * tap : 128 * tap + 128] = jnp.transpose(uconv_v[s, tap].astype(F32)).astype(BF16)

    copies[at["btime"]].wait()
    emb_b = dot(code_base, btime_v[...])
    w_in = b_in[...]
    for m in range(2):
        rolled = pltpu.roll(x8b[m], jnp.mod(32 - 256 * z, 1024), 1)
        own_t = jnp.transpose(rolled[:, 0:384])[0:320, :]
        blk_t = jnp.transpose(x8b[m, :, 0:384])[0:288, :].reshape(9, 32, 8)[:, 0:16, :].reshape(144, 8)
        pix = jnp.concatenate([own_t, blk_t], axis=0)[:, 0:3].astype(BF16)
        hidden = dot(pix, w_in) + emb_b[m : m + 1, :]
        scale = lax.rsqrt(jnp.mean(hidden * hidden, axis=-1, keepdims=True) + 1e-6)
        half = hidden * scale * (b_gain[0:1, :] * 0.5)
        active = half + half * jnp.tanh(half)
        hid[256 * m : 256 * m + 256, :] = hidden[32:288]
        hid[512 + 64 * m : 576 + 64 * m, :] = hidden[320:464].reshape(9, 16, 512)[0:8, 0:8].reshape(64, 512)
        own = active[0:320]
        line = iota((320, 1), 0)
        gone = ((line < 32) & (z == 0)) | ((line >= 288) & (z == SEG - 1))
        own = jnp.where(gone, 0.0, own)
        blk = active[320:464]
        col = line % 32
        bcol = iota((144, 1), 0) % 16
        for b in range(3):
            if b == 0:
                mine = jnp.where(col == 0, 0.0, pltpu.roll(own, 1, 0))
                near = jnp.where(bcol == 0, 0.0, pltpu.roll(blk, 1, 0))
            elif b == 1:
                mine, near = own, blk
            else:
                mine = jnp.where(col == 31, 0.0, pltpu.roll(own, 319, 0))
                near = pltpu.roll(blk, 143, 0)
            mine = mine.astype(BF16)
            near = near.reshape(9, 16, 512)[:, 0:8].reshape(72, 512)
            near = jnp.concatenate([jnp.zeros((8, 512), F32), near], axis=0)
            for a in range(3):
                taps[256 * m : 256 * m + 256, 512 * (3 * a + b) : 512 * (3 * a + b) + 512] = mine[32 * a : 32 * a + 256]
                taps[512 + 64 * m : 576 + 64 * m, 512 * (3 * a + b) : 512 * (3 * a + b) + 512] = near[8 * a : 8 * a + 64].astype(BF16)

    copies[at["text"]].wait()

    copies[at["bconv"]].wait()

    for i in range(4):
        states = text_v[64 * i : 64 * i + 64, :].astype(F32)
        scale = lax.rsqrt(jnp.mean(states * states, axis=-1, keepdims=True) + 1e-6)
        ctx[64 * i : 64 * i + 64, :] = (states * scale * t5g[...]).astype(BF16)

    hid[...] += dot(taps[...], bconv_v[...])

    copies[at["noise"]].wait()
    packed = jnp.zeros((LANE * 24, 128), F32)
    for m in range(2):
        rows = noise_v[m].astype(F32)
        for half in range(2):
            group = 2 * m + half
            place_at = (iota((32, 128), 0) + 32 * group == iota((32, 128), 1)).astype(F32).astype(BF16)
            packed += dot(rows[:, :, 8 * half : 8 * half + 8, :].reshape(LANE * 24, 32).astype(BF16), place_at)
    snd[:, 0:24, :] = packed.reshape(LANE, 24, 128)
    snd[:, 24:32, :] = jnp.zeros((LANE, 8, 128), F32)
    snd_b[...] = snd[...].astype(BF16)

    lower = (k == LANE - 1) & (y < SEG - 1)
    upper = (k == 0) & (y > 0)
    extra = jnp.where(lower | upper, LANE, 0)
    pl.semaphore_wait(barrier, LANE - 1 + jnp.where(y != z, 1, 0) + extra)

    def noise_to(j, slot):
        return remote(snd_b.at[j], rcv.at[slot], send.at[j], recv.at[slot], y, z * LANE + j)

    def halo_to(j, slot, to):
        return remote(snd_b.at[j], rcv.at[slot], halo_send.at[j], recv.at[slot], to, z * LANE + j)

    each_other(z, y, k, lambda j: noise_to(j, k).start())
    for cond, slot, step in ((lower, LANE, 1), (upper, LANE + 1, -1)):
        @pl.when(cond)
        def _():
            for j in range(LANE):
                halo_to(j, slot, y + step).start()

    @pl.when(y == z)
    def _():
        rcv[k] = snd_b[k]

    for n in range(3):
        copies[at["kv"] + n].wait()
        if n == 2:
            copies[at["kv"] + 3].wait()
        kv[:, 512 * n : 512 * n + 512] = dot(ctx[...], kv_w[n]).astype(BF16)

    for s in range(2):
        for m in range(2):
            key = kv[128 * m : 128 * m + 128, 1024 + 256 * s : 1152 + 256 * s]
            val = jnp.transpose(kv[128 * m : 128 * m + 128, 1152 + 256 * s : 1280 + 256 * s].astype(F32)).astype(BF16)
            zero = jnp.zeros_like(key)
            kcat[2 * s + m, 0:128, :] = jnp.where(lane128 < 64, key, zero)
            kcat[2 * s + m, 128:256, :] = jnp.where(lane128 < 64, zero, key)
            vcat[2 * s + m, 0:128, 0:128] = jnp.where(sub128 < 64, val, zero)
            vcat[2 * s + m, 0:128, 128:256] = jnp.where(sub128 < 64, zero, val)
            head_of = iota((16, 256), 1) // 128
            vcat[2 * s + m, 128:144, :] = (head_of == iota((16, 256), 0)).astype(F32).astype(BF16)

    copies[at["bq"]].wait()
    copies[at["bo"]].wait()
    h2 = hid[...]
    scale = lax.rsqrt(jnp.mean(h2 * h2, axis=-1, keepdims=True) + 1e-6)
    query[...] = (dot((h2 * scale * b_gain[1:2, :]).astype(BF16), bq_v[...]) * SCALE).astype(BF16)
    for m in range(2):
        for pair in range(4):
            lo = 128 * pair
            key = kv[128 * m : 128 * m + 128, lo : lo + 128]
            val = kv[128 * m : 128 * m + 128, 512 + lo : 640 + lo]
            zero = jnp.zeros_like(key)
            keys = jnp.concatenate([jnp.where(lane128 < 64, key, zero), jnp.where(lane128 < 64, zero, key)], axis=0)
            vals = jnp.concatenate([jnp.where(lane128 < 64, val, zero), jnp.where(lane128 < 64, zero, val)], axis=0)
            ones = ((iota((256, 128), 0) < 128) == (iota((256, 128), 1) < 64)).astype(F32).astype(BF16)
            vals = jnp.concatenate([vals, ones], axis=1)
            q = jnp.concatenate(
                [query[256 * m : 256 * m + 256, lo : lo + 128], query[512 + 64 * m : 576 + 64 * m, lo : lo + 128]], axis=0
            )
            score = dot_nt(q, keys) + mask_row[m]
            left, right = score[:, 0:128], score[:, 128:256]
            left = jnp.exp2(left - jnp.max(left, axis=-1, keepdims=True))
            right = jnp.exp2(right - jnp.max(right, axis=-1, keepdims=True))
            mixed = dot(jnp.concatenate([left, right], axis=1).astype(BF16), vals)
            mixed = (mixed[:, 0:128] / mixed[:, 128:256]).astype(BF16)
            att[256 * m : 256 * m + 256, lo : lo + 128] = mixed[0:256]
            att[512 + 64 * m : 576 + 64 * m, lo : lo + 128] = mixed[256:320]
    h3 = hid[...] + dot(att[...], bo_v[...])
    scale = lax.rsqrt(jnp.mean(h3 * h3, axis=-1, keepdims=True) + 1e-6)
    eps = dot_nt(head8[...].astype(BF16), (h3 * scale * b_gain[2:3, :]).astype(BF16))

    def step_of(noisy, eps, c0, c1, c2_, c3):
        c0, c1, c2_, c3 = (jnp.concatenate([c] * (eps.shape[1] // 128), axis=1) for c in (c0, c1, c2_, c3))
        clean = jnp.clip((noisy - c0 * eps) * c1, -1.0, 1.0)
        return clean, c2_ * clean + c3 * eps

    pick_k, pick_l = iota((256, 128), 0), iota((256, 128), 1)
    noisy = jnp.zeros((8, 128), F32)
    for m in range(2):
        whole = pltpu.roll(x8b[m], jnp.mod(0 - 256 * z, 1024), 1)[:, 0:256]
        _, prior = step_of(whole, eps[:, 256 * m : 256 * m + 256], *coefs(0, m))
        for c in range(3):
            early_v[0, c, m : m + 1, :] = prior[c : c + 1]
        spot = pick_l - 64 * m
        sel = (spot >= 0) & (spot < 64) & ((pick_k >> 5) == (spot >> 3)) & ((pick_k & 31) == (spot & 7))
        noisy += dot(x8b[m, :, 0:256].astype(BF16), sel.astype(F32).astype(BF16))
    first_half = iota((8, 128), 1) < 64
    mixed_coefs = tuple(jnp.where(first_half, a, b) for a, b in zip(coefs(0, 0), coefs(0, 1)))
    region, _ = step_of(noisy, eps[:, 512:640], *mixed_coefs)
    region = region.astype(BF16)

    def back(s, ms, h2, width):
        scale = lax.rsqrt(jnp.sum(h2 * h2, axis=0, keepdims=True) * (1.0 / 128.0) + 1e-6)
        q = (dot(wq_t[s], h2.astype(BF16)) * scale).astype(BF16)
        both = []
        for n, m in enumerate(ms):
            score = dot(kcat[2 * s + m], q[:, width * n : width * n + width])
            mask = jnp.concatenate([mask_col[m]] * (width // 128), axis=1)
            left, right = score[0:128] + mask, score[128:256] + mask
            left = jnp.exp2(left - jnp.max(left, axis=0, keepdims=True)).astype(BF16)
            right = jnp.exp2(right - jnp.max(right, axis=0, keepdims=True)).astype(BF16)
            mixed = dot(vcat[2 * s + m], jnp.concatenate([left, right], axis=0))
            top = mixed[0:64] * (1.0 / mixed[128:129])
            bottom = mixed[64:128] * (1.0 / mixed[129:130])
            both.append(jnp.concatenate([top, bottom], axis=0).astype(BF16))
        both = both[0] if len(both) == 1 else jnp.concatenate(both, axis=1)
        h3 = h2 + dot(wo_t[s], both)
        scale = lax.rsqrt(jnp.sum(h3 * h3, axis=0, keepdims=True) * (1.0 / 128.0) + 1e-6)
        return dot(wh_t[s], h3.astype(BF16)) * scale

    def activate(hidden, s, width):
        scale = lax.rsqrt(jnp.sum(hidden * hidden, axis=0, keepdims=True) * (1.0 / 128.0) + 1e-6)
        gain = jnp.concatenate([gcol[s]] * (width // 128), axis=1)
        half = hidden * scale * gain
        return half + half * jnp.tanh(half)

    lane1 = iota((1, 128), 1)

    def regroup(value, source, target):
        by = 32 * (target - source) % 128
        return pltpu.roll(value, by, 1) if by else value

    lanes = iota((1, 768), 1)
    lanes = jnp.where(lanes >= 384, lanes - 384, lanes)
    row_of = 8 * z - 2 + (lanes >> 5)
    col_of = lanes & 31
    inside = (row_of >= 0) & (row_of < 32)
    spread_k = iota((128, 384), 0)
    spread_l = iota((128, 384), 1)
    spread_at = (((8 * z + 2 + (spread_l >> 5)) >> 2) - 1) * 8 + ((spread_l & 31) >> 2)
    spread_at = jnp.where((spread_at >= 0) & (spread_at < 64), spread_at, -1000)
    which = iota((8, 384), 0)
    noisy, hidden = [], []
    for m in range(2):
        x = pltpu.roll(x8u[m], jnp.mod(64 - 256 * z, 1024), 1)[:, 0:384]
        cond = pltpu.roll(dot(region, (spread_k == spread_at + 64 * m).astype(F32).astype(BF16)), 3, 0)
        x8 = jnp.where(which < 3, x, jnp.where(which < 6, cond, 1.0))
        hidden.append(dot(gcol[2 + m, :, 0:8].astype(BF16), x8.astype(BF16)))
        noisy.append(x)
    hidden = jnp.concatenate(hidden, axis=1)
    active = jnp.where(inside, activate(hidden, 0, 768), 0.0)
    stack = [
        jnp.where(col_of == 0, 0.0, pltpu.roll(active, 1, 1)),
        active,
        jnp.where(col_of == 31, 0.0, pltpu.roll(active, 767, 1)),
    ]
    stack = [pltpu.roll(one, 32, 1) for one in stack] + stack + [pltpu.roll(one, 736, 1) for one in stack]
    stack = jnp.concatenate([one.astype(BF16) for one in stack], axis=0)
    eps = back(0, (0, 1), hidden + dot(conv_t[0], stack), 384)
    for m in range(2):
        clean, prior = step_of(noisy[m], eps[:, 384 * m : 384 * m + 384], *coefs(1, m))
        prior = pltpu.roll(prior, 320, 1)[:, 0:256]
        for c in range(3):
            early_v[1, c, m : m + 1, :] = prior[c : c + 1]
        clean = clean.astype(BF16).astype(F32)

        def rows_at(first):
            total = None
            for g in range(4):
                row = first + 2 * g
                one = regroup(clean[:, 128 * (row // 4) : 128 * (row // 4) + 128], row % 4, g)
                total = one if total is None else jnp.where((lane1 >> 5) == g, one, total)
            return total

        x2[m] = jnp.ones((34 * 8, 128), F32)
        even, odd = rows_at(2), rows_at(3)
        above, below = rows_at(1), rows_at(4)
        for c in range(3):
            x2[m, pl.ds(8 + 3 + c, 16, 8), :] = jnp.broadcast_to(even[c : c + 1], (16, 128))
            x2[m, pl.ds(8 * 17 + 3 + c, 16, 8), :] = jnp.broadcast_to(odd[c : c + 1], (16, 128))
            x2[m, 3 + c : 4 + c, :] = above[c : c + 1]
            x2[m, 33 * 8 + 3 + c : 33 * 8 + 4 + c, :] = below[c : c + 1]

    early[...] = early_v[...].astype(BF16)
    each_other(z, y, k, lambda j: noise_to(j, j).wait_recv())

    @pl.when(z > 0)
    def _():
        noise_to(0, LANE).wait_recv()

    @pl.when(z < SEG - 1)
    def _():
        noise_to(0, LANE + 1).wait_recv()

    @pl.when(z == 0)
    def _():
        rcv[LANE] = jnp.zeros((32, 128), BF16)

    @pl.when(z == SEG - 1)
    def _():
        rcv[LANE + 1] = jnp.zeros((32, 128), BF16)

    blocks = [rcv[n].astype(F32)[0:24] for n in range(LANE + 2)]
    for m in range(2):
        edge = {}
        for h in range(2):
            for half in range(2):
                group = 2 * m + half
                total = regroup(blocks[h], group, 0)
                for g in range(1, 4):
                    total = jnp.where((lane1 >> 5) == g, regroup(blocks[2 * g + h], group, g), total)
                edge[h, half] = total
                for c in range(3):
                    x2[m, pl.ds(8 * (1 + 16 * h + 8 * half) + c, 8, 8), :] = total[8 * c : 8 * c + 8]
        top = regroup(blocks[LANE], 2 * m + 1, 0)
        low = regroup(blocks[LANE + 1], 2 * m, 3)
        over = pltpu.roll(edge[1, 1], 32, 1)
        under = pltpu.roll(edge[0, 0], 96, 1)
        for c in range(3):
            x2[m, c : c + 1, :] = jnp.where(lane1 < 32, top, over)[8 * c + 7 : 8 * c + 8]
            x2[m, 33 * 8 + c : 33 * 8 + c + 1, :] = jnp.where(lane1 >= 96, low, under)[8 * c : 8 * c + 1]

    def result_to(m, j, slot):
        return remote(snd2.at[m, j], rcv2.at[m, slot], send2.at[m, j], recv2.at[m, slot], y, z * LANE + j)

    FT = 17
    lanef = iota((1, 128 * FT), 1)
    colf = iota((1, 128), 1) & 31
    for m in range(2):
        for n in range(34 // FT):
            t = n * FT
            rows = x2[m, t * 8 : (t + FT) * 8, :]
            x8 = jnp.concatenate([rows[8 * e : 8 * e + 8] for e in range(FT)], axis=1).astype(BF16)
            hidden = dot(gcol[4 + m, :, 0:8].astype(BF16), x8)
            active = activate(hidden, 1, 128 * FT)
            if n == 0:
                active = jnp.where((lanef < 32) & (z == 0), 0.0, active)
            else:
                active = jnp.where((lanef >= 128 * FT - 32) & (z == SEG - 1), 0.0, active)
            for h in range(FT):
                one = active[:, 128 * h : 128 * h + 128]
                hid3[m, t + h] = hidden[:, 128 * h : 128 * h + 128]
                act3[m, t + h, 0:128] = jnp.where(colf == 0, 0.0, pltpu.roll(one, 1, 1)).astype(BF16)
                act3[m, t + h, 128:256] = one.astype(BF16)
                act3[m, t + h, 256:384] = jnp.where(colf == 31, 0.0, pltpu.roll(one, 127, 1)).astype(BF16)

        for i in range(0, 32, STEPS):
            tiles = [act3[m, i + e] for e in range(STEPS + 2)]
            stack = jnp.concatenate(
                [jnp.concatenate(tiles[a : a + STEPS], axis=1) for a in range(3)], axis=0
            )
            h2 = jnp.concatenate([hid3[m, i + 1 + e] for e in range(STEPS)], axis=1) + dot(conv_t[1], stack)
            eps = back(1, (m,), h2, 128 * STEPS)
            rows = x2[m, (i + 1) * 8 : (i + 1 + STEPS) * 8, :]
            noisy = jnp.concatenate([rows[8 * e : 8 * e + 8] for e in range(STEPS)], axis=1)
            clean, prior = step_of(noisy, eps, *coefs(2, m))
            for e in range(STEPS):
                c2[0, m, (i + e) * 8 : (i + e) * 8 + 8, :] = clean[:, 128 * e : 128 * e + 128]
                c2[1, m, (i + e) * 8 : (i + e) * 8 + 8, :] = prior[:, 128 * e : 128 * e + 128]

        for j in range(LANE):
            rows = []
            for c in range(3):
                total = None
                for o in range(2):
                    for half in range(2):
                        one = c2[o, m, pl.ds(128 * (j % 2) + 64 * half + c, 8, 8), :]
                        one = regroup(one, j // 2, 2 * o + half)
                        total = one if total is None else jnp.where((lane1 >> 5) == 2 * o + half, one, total)
                rows.append(total)
            rows.append(jnp.zeros((8, 128), F32))
            snd2[m, j] = jnp.concatenate(rows, axis=0).astype(BF16)

        each_other(z, y, k, lambda j: result_to(m, j, k).start())

        @pl.when(y == z)
        def _():
            rcv2[m, k] = snd2[m, k]

    each_other(z, y, k, lambda j: noise_to(j, k).wait_send())
    for cond, slot, step in ((lower, LANE, 1), (upper, LANE + 1, -1)):
        @pl.when(cond)
        def _():
            for j in range(LANE):
                halo_to(j, slot, y + step).wait_send()

    for m in range(2):
        each_other(z, y, k, lambda j: result_to(m, j, j).wait_recv())
    for m in range(2):
        each_other(z, y, k, lambda j: result_to(m, j, k).wait_send())


def unpack_kernel(early_in, got, early, out):
    early[...] = early_in[...]
    for m in range(2):
        for j in range(LANE):
            whole = got[m, j].astype(F32)[0:24]
            for o in range(2):
                upper, lower = (
                    pltpu.roll(whole, (128 - 32 * (2 * o + half)) % 128, 1)[:, 0:32] if 2 * o + half else whole[:, 0:32]
                    for half in range(2)
                )
                for c in range(3):
                    both = jnp.concatenate([upper[8 * c : 8 * c + 8], lower[8 * c : 8 * c + 8]], axis=0)
                    out[o, m, j, c] = both.astype(BF16)


def shards(
    text_states, token_ids, step_ids, base_noise, upscale_noise, final_noise, t5_gain,
    base_keyval, upscale_keyval, base_input, base_time, base_gain, base_conv, base_query,
    base_output, base_head, upscale_input, upscale_time, upscale_gain, upscale_conv,
    upscale_query, upscale_output, upscale_head,
):
    early, got = pl.pallas_call(
        step_kernel,
        out_shape=(
            jax.ShapeDtypeStruct((2, 3, 2, 256), BF16),
            jax.ShapeDtypeStruct((2, LANE, 32, 128), BF16),
        ),
        in_specs=[SMEM] + [VMEM] * 10 + [ANY] * 12,
        out_specs=(VMEM, VMEM),
        scratch_shapes=[
            pltpu.VMEM((256, 4096), BF16),
            pltpu.VMEM((3, 4096, 512), BF16),
            pltpu.VMEM((512, 512), BF16),
            pltpu.VMEM((4608, 512), BF16),
            pltpu.VMEM((512, 512), BF16),
            pltpu.VMEM((512, 512), BF16),
            pltpu.VMEM((2, 128, 128), BF16),
            pltpu.VMEM((2, 9, 128, 128), BF16),
            pltpu.VMEM((2, 128, 128), BF16),
            pltpu.VMEM((2, 128, 128), BF16),
            pltpu.VMEM((2, LANE, 3, 16, 32), BF16),
            pltpu.VMEM((256, 4096), BF16),
            pltpu.VMEM((256, 1536), BF16),
            pltpu.VMEM((640, 4608), BF16),
            pltpu.VMEM((640, 512), F32),
            pltpu.VMEM((640, 512), BF16),
            pltpu.VMEM((640, 512), BF16),
            pltpu.VMEM((2, 8, 1024), F32),
            pltpu.VMEM((2, 8, 1024), F32),
            pltpu.VMEM((8, 128), F32),
            pltpu.VMEM((8, 128), F32),
            pltpu.VMEM((6, 128, 128), F32),
            pltpu.VMEM((2, 128, 128), BF16),
            pltpu.VMEM((2, 128, 128), BF16),
            pltpu.VMEM((2, 8, 128), BF16),
            pltpu.VMEM((2, 128, 1152), BF16),
            pltpu.VMEM((4, 256, 128), BF16),
            pltpu.VMEM((4, 144, 256), BF16),
            pltpu.VMEM((2, 1, 256), F32),
            pltpu.VMEM((2, 128, 128), F32),
            pltpu.VMEM((8, 512), F32),
            pltpu.VMEM((2, 272, 128), F32),
            pltpu.VMEM((2, 34, 128, 128), F32),
            pltpu.VMEM((2, 34, 384, 128), BF16),
            pltpu.VMEM((2, 2, 256, 128), F32),
            pltpu.VMEM((2, 3, 2, 256), F32),
            pltpu.VMEM((LANE, 32, 128), F32),
            pltpu.VMEM((LANE, 32, 128), BF16),
            pltpu.VMEM((LANE + 2, 32, 128), BF16),
            pltpu.VMEM((2, LANE, 32, 128), BF16),
            pltpu.SemaphoreType.DMA((14,)),
            pltpu.SemaphoreType.DMA((LANE,)),
            pltpu.SemaphoreType.DMA((LANE + 2,)),
            pltpu.SemaphoreType.DMA((LANE,)),
            pltpu.SemaphoreType.DMA((2, LANE)),
            pltpu.SemaphoreType.DMA((2, LANE)),
        ],
        compiler_params=pltpu.CompilerParams(
            vmem_limit_bytes=56 * 1024 * 1024, collective_id=0, has_side_effects=True
        ),
        name="denoise",
    )(
        step_ids.T, token_ids, base_noise[:, 0].transpose(1, 0, 2), upscale_noise[:, 0].transpose(1, 0, 2), t5_gain[None],
        base_input, base_gain, base_head.T, upscale_input.transpose(1, 0, 2), upscale_gain.transpose(1, 0, 2),
        upscale_head.transpose(2, 0, 1), final_noise,
        text_states.reshape(256, 4096), base_keyval, upscale_keyval, base_time, base_conv.reshape(4608, 512),
        base_query, base_output, upscale_time, upscale_conv, upscale_query, upscale_output,
    )
    early, final_states = pl.pallas_call(
        unpack_kernel,
        out_shape=(
            jax.ShapeDtypeStruct((2, 3, 2, 256), BF16),
            jax.ShapeDtypeStruct((2, 2, LANE, 3, 16, 32), BF16),
        ),
        in_specs=[VMEM] * 2,
        out_specs=(VMEM, VMEM),
        compiler_params=pltpu.CompilerParams(vmem_limit_bytes=60 * 1024 * 1024),
        name="unpack",
    )(early, got)
    return early.transpose(0, 2, 1, 3)[:, :, None], final_states


def solution(mesh):
    placed = [P() for _ in range(23)]
    placed[0] = placed[3] = placed[4] = P(None, "space", None, None)
    placed[5] = P(None, None, None, "space", None)
    return jax.shard_map(
        shards,
        mesh=mesh,
        in_specs=tuple(placed),
        out_specs=(
            P(None, None, "space", None, "segment"),
            P(None, None, "segment", None, "space", None),
        ),
        check_vma=False,
    )
```

```python
import functools
import math

import jax
import jax.numpy as jnp
from jax import lax
from jax.experimental import pallas as pl
from jax.experimental.pallas import tpu as pltpu
from jax.sharding import PartitionSpec as P

MESH = pl.DeviceIdType.MESH
ANY = pl.BlockSpec(memory_space=pl.ANY)
VMEM = pl.BlockSpec(memory_space=pltpu.VMEM)
SMEM = pl.BlockSpec(memory_space=pltpu.SMEM)
F32, BF16 = jnp.float32, jnp.bfloat16
LOG2E = 1.4426950408889634
SCALE = 0.125 * LOG2E
SEG, LANE = 4, 8

STEPS = 32


def dot(a, b):
    return jnp.dot(a, b, preferred_element_type=F32)


def dot_nt(a, b):
    return lax.dot_general(a, b, (((1,), (1,)), ((), ())), preferred_element_type=F32)


def iota(shape, dim):
    return lax.broadcasted_iota(jnp.int32, shape, dim)


def place():
    z = lax.axis_index("segment")
    p = lax.axis_index("space")
    return z, p // LANE, p % LANE


def remote(src, dst, send, recv, z, p):
    return pltpu.make_async_remote_copy(
        src_ref=src, dst_ref=dst, send_sem=send, recv_sem=recv, device_id=(z, p), device_id_type=MESH
    )


def each_other(z, y, k, body):
    for j in range(LANE):
        @pl.when((y != z) | (k != j))
        def _():
            body(j)


def step_kernel(
    steps, ids, bx, ux, t5g, b_in, b_gain, b_head, u_in, u_gain, u_head,
    noise_h, text_h, bkv_h, ukv_h, btime_h, bconv_h, bq_h, bo_h, utime_h, uconv_h, uq_h, uo_h,
    early, rcv2,
    text_v, kv_w, btime_v, bconv_v, bq_v, bo_v, utime_v, uconv_v, uq_v, uo_v, noise_v,
    ctx, kv, taps, hid, query, att, x8b, x8u, rows8, aug8, gcol, wq_t, wo_t, wh_t, conv_t,
    kcat, vcat, mask_row, mask_col, head8, x2, hid3, act3, c2, early_v,
    snd, snd_b, rcv, snd2, sems, send, recv, halo_send, send2, recv2, own_sems,
):
    z, y, k = place()
    p = y * LANE + k

    barrier = pltpu.get_barrier_semaphore()

    def hello(z_to, p_to):
        pl.semaphore_signal(barrier, inc=1, device_id=(z_to, p_to), device_id_type=MESH)

    each_other(z, y, k, lambda j: hello(y, z * LANE + j))

    @pl.when(z > 0)
    def _():
        hello(y, z * LANE - 1)

    @pl.when(z < SEG - 1)
    def _():
        hello(y, z * LANE + LANE)

    copies = [
        pltpu.make_async_copy(src, dst, sems.at[n])
        for n, (src, dst) in enumerate(
            [
                (utime_h, utime_v), (uq_h, uq_v), (uo_h, uo_v), (uconv_h, uconv_v), (btime_h, btime_v),
                (text_h, text_v), (noise_h.at[:, pl.ds(z * LANE, LANE)], noise_v),
            ]
            + [(bconv_h.at[1536 * n : 1536 * n + 1536], bconv_v.at[1536 * n : 1536 * n + 1536]) for n in range(3)]
            + [(bkv_h.at[:, 512 * n : 512 * n + 512], kv_w.at[n]) for n in range(2)]
            + [(ukv_h.at[n], kv_w.at[2, :, 256 * n : 256 * n + 256]) for n in range(2)]
            + [(bq_h, bq_v), (bo_h, bo_v)]
        )
    ]
    for copy in copies:
        copy.start()
    at = dict(utime=0, uq=1, uo=2, uconv=3, btime=4, text=5, noise=6, bconv=7, kv=10, bq=14, bo=15)

    lane128 = iota((128, 128), 1)
    sub128 = iota((128, 128), 0)
    for m in range(2):
        x8b[m] = jnp.zeros((8, 1024), F32)
        x8u[m] = jnp.zeros((8, 1024), F32)
        for c in range(3):
            x8b[m, c : c + 1, :] = bx[c].astype(F32)[m : m + 1]
            x8u[m, c : c + 1, :] = ux[c].astype(F32)[m : m + 1]
        row = jnp.where(ids[m, pl.ds(p, 1), :] != 0, 0.0, -1e30)
        mask_row[m, :, 0:128] = row
        mask_row[m, :, 128:256] = row
        rows8[...] = jnp.broadcast_to(row, (8, 128))
        column = jnp.transpose(rows8[...])[:, 0:1]
        mask_col[m] = jnp.broadcast_to(column, (128, 128))
    head8[...] = jnp.zeros_like(head8)
    head8[0:3, :] = b_head[...].astype(F32)

    def code(width, first):
        row, lane = iota((8, width), 0), iota((8, width), 1)
        step = jnp.zeros((8, width), F32)
        for s in range(2):
            for m in range(2):
                section = min(first + s, 2)
                step = jnp.where(row == 2 * s + m, steps[m, section].astype(F32), step)
        half = width // 2
        angle = step * jnp.exp((-math.log(10000.0) / half) * (lane % half).astype(F32))
        return jnp.where(lane < half, jnp.sin(angle), jnp.cos(angle)).astype(BF16)

    def coefs(s, m):
        step = jnp.full((8, 128), steps[m, s].astype(F32))

        def alpha(at_step):
            return jnp.cos((at_step / 1000.0 + 0.008) * (math.pi / 2 / 1.008)) ** 2

        level, earlier = alpha(step), alpha(step - 50.0)
        return jnp.sqrt(1.0 - level), 1.0 / jnp.sqrt(level), jnp.sqrt(earlier), jnp.sqrt(1.0 - earlier)

    for n in range(4):
        copies[n].wait()
    code_up = code(128, 1)
    code_base = code(512, 0)
    for s in range(2):
        emb = dot(code_up, utime_v[s])
        for m in range(2):
            for c in range(6):
                aug8[c : c + 1, :] = u_in[c].astype(F32)[s : s + 1]
            one = emb[2 * s + m : 2 * s + m + 1, :]
            high = one.astype(BF16).astype(F32)
            aug8[6:7, :] = high
            aug8[7:8, :] = one - high
            x8 = jnp.transpose(aug8[...]).astype(BF16)
            gcol[2 + 2 * s + m, :, 0:8] = x8.astype(F32)
        rows8[...] = jnp.zeros((8, 128), F32)
        for c in range(3):
            rows8[c : c + 1, :] = u_gain[c, s : s + 1, :]
        turned = jnp.transpose(rows8[...])
        gcol[s] = jnp.broadcast_to(turned[:, 0:1] * 0.5, (128, 128))
        wq_t[s] = jnp.transpose(uq_v[s].astype(F32) * (turned[:, 1:2] * SCALE)).astype(BF16)
        wo_t[s] = jnp.transpose(uo_v[s].astype(F32)).astype(BF16)
        rows8[...] = jnp.zeros((8, 128), F32)
        for c in range(3):
            rows8[c : c + 1, :] = u_head[c].astype(F32)[s : s + 1] * u_gain[2, s : s + 1, :]
        wh_t[s] = rows8[...].astype(BF16)
        for tap in range(9):
            conv_t[s, :, 128 * tap : 128 * tap + 128] = jnp.transpose(uconv_v[s, tap].astype(F32)).astype(BF16)

    copies[at["btime"]].wait()
    emb_b = dot(code_base, btime_v[...])
    w_in = b_in[...]
    for m in range(2):
        rolled = pltpu.roll(x8b[m], jnp.mod(32 - 256 * z, 1024), 1)
        own_t = jnp.transpose(rolled[:, 0:384])[0:320, :]
        blk_t = jnp.transpose(x8b[m, :, 0:384])[0:288, :].reshape(9, 32, 8)[:, 0:16, :].reshape(144, 8)
        pix = jnp.concatenate([own_t, blk_t], axis=0)[:, 0:3].astype(BF16)
        hidden = dot(pix, w_in) + emb_b[m : m + 1, :]
        scale = lax.rsqrt(jnp.mean(hidden * hidden, axis=-1, keepdims=True) + 1e-6)
        half = hidden * scale * (b_gain[0:1, :] * 0.5)
        active = half + half * jnp.tanh(half)
        hid[256 * m : 256 * m + 256, :] = hidden[32:288]
        hid[512 + 64 * m : 576 + 64 * m, :] = hidden[320:464].reshape(9, 16, 512)[0:8, 0:8].reshape(64, 512)
        own = active[0:320]
        line = iota((320, 1), 0)
        gone = ((line < 32) & (z == 0)) | ((line >= 288) & (z == SEG - 1))
        own = jnp.where(gone, 0.0, own)
        blk = active[320:464]
        col = line % 32
        bcol = iota((144, 1), 0) % 16
        for b in range(3):
            if b == 0:
                mine = jnp.where(col == 0, 0.0, pltpu.roll(own, 1, 0))
                near = jnp.where(bcol == 0, 0.0, pltpu.roll(blk, 1, 0))
            elif b == 1:
                mine, near = own, blk
            else:
                mine = jnp.where(col == 31, 0.0, pltpu.roll(own, 319, 0))
                near = pltpu.roll(blk, 143, 0)
            mine = mine.astype(BF16)
            near = near.reshape(9, 16, 512)[:, 0:8].reshape(72, 512)
            near = jnp.concatenate([jnp.zeros((8, 512), F32), near], axis=0)
            for a in range(3):
                taps[256 * m : 256 * m + 256, 512 * (3 * a + b) : 512 * (3 * a + b) + 512] = mine[32 * a : 32 * a + 256]
                taps[512 + 64 * m : 576 + 64 * m, 512 * (3 * a + b) : 512 * (3 * a + b) + 512] = near[8 * a : 8 * a + 64].astype(BF16)

    copies[at["text"]].wait()

    for i in range(4):
        states = text_v[64 * i : 64 * i + 64, :].astype(F32)
        scale = lax.rsqrt(jnp.mean(states * states, axis=-1, keepdims=True) + 1e-6)
        ctx[64 * i : 64 * i + 64, :] = (states * scale * t5g[...]).astype(BF16)

    for n in range(3):
        copies[at["bconv"] + n].wait()
        hid[...] += dot(taps[:, 1536 * n : 1536 * n + 1536], bconv_v[1536 * n : 1536 * n + 1536, :])

    copies[at["noise"]].wait()
    packed = jnp.zeros((LANE * 24, 128), F32)
    for m in range(2):
        rows = noise_v[m].astype(F32)
        for half in range(2):
            group = 2 * m + half
            place_at = (iota((32, 128), 0) + 32 * group == iota((32, 128), 1)).astype(F32).astype(BF16)
            packed += dot(rows[:, :, 8 * half : 8 * half + 8, :].reshape(LANE * 24, 32).astype(BF16), place_at)
    snd[:, 0:24, :] = packed.reshape(LANE, 24, 128)
    snd[:, 24:32, :] = jnp.zeros((LANE, 8, 128), F32)
    snd_b[...] = snd[...].astype(BF16)

    lower = (k == LANE - 1) & (y < SEG - 1)
    upper = (k == 0) & (y > 0)
    extra = jnp.where(lower | upper, LANE, 0)
    pl.semaphore_wait(barrier, LANE - 1 + jnp.where(y != z, 1, 0) + extra)

    def noise_to(j, slot):
        return remote(snd_b.at[j], rcv.at[slot], send.at[j], recv.at[slot], y, z * LANE + j)

    def halo_to(j, slot, to):
        return remote(snd_b.at[j], rcv.at[slot], halo_send.at[j], recv.at[slot], to, z * LANE + j)

    each_other(z, y, k, lambda j: noise_to(j, k).start())
    for cond, slot, step in ((lower, LANE, 1), (upper, LANE + 1, -1)):
        @pl.when(cond)
        def _():
            for j in range(LANE):
                halo_to(j, slot, y + step).start()

    @pl.when(y == z)
    def _():
        rcv[k] = snd_b[k]

    for n in range(3):
        copies[at["kv"] + n].wait()
        if n == 2:
            copies[at["kv"] + 3].wait()
        kv[:, 512 * n : 512 * n + 512] = dot(ctx[...], kv_w[n]).astype(BF16)

    for s in range(2):
        for m in range(2):
            key = kv[128 * m : 128 * m + 128, 1024 + 256 * s : 1152 + 256 * s]
            val = jnp.transpose(kv[128 * m : 128 * m + 128, 1152 + 256 * s : 1280 + 256 * s].astype(F32)).astype(BF16)
            zero = jnp.zeros_like(key)
            kcat[2 * s + m, 0:128, :] = jnp.where(lane128 < 64, key, zero)
            kcat[2 * s + m, 128:256, :] = jnp.where(lane128 < 64, zero, key)
            vcat[2 * s + m, 0:128, 0:128] = jnp.where(sub128 < 64, val, zero)
            vcat[2 * s + m, 0:128, 128:256] = jnp.where(sub128 < 64, zero, val)
            head_of = iota((16, 256), 1) // 128
            vcat[2 * s + m, 128:144, :] = (head_of == iota((16, 256), 0)).astype(F32).astype(BF16)

    copies[at["bq"]].wait()
    copies[at["bo"]].wait()
    h2 = hid[...]
    scale = lax.rsqrt(jnp.mean(h2 * h2, axis=-1, keepdims=True) + 1e-6)
    query[...] = (dot((h2 * scale * b_gain[1:2, :]).astype(BF16), bq_v[...]) * SCALE).astype(BF16)
    for m in range(2):
        for pair in range(4):
            lo = 128 * pair
            key = kv[128 * m : 128 * m + 128, lo : lo + 128]
            val = kv[128 * m : 128 * m + 128, 512 + lo : 640 + lo]
            zero = jnp.zeros_like(key)
            keys = jnp.concatenate([jnp.where(lane128 < 64, key, zero), jnp.where(lane128 < 64, zero, key)], axis=0)
            vals = jnp.concatenate([jnp.where(lane128 < 64, val, zero), jnp.where(lane128 < 64, zero, val)], axis=0)
            ones = ((iota((256, 128), 0) < 128) == (iota((256, 128), 1) < 64)).astype(F32).astype(BF16)
            vals = jnp.concatenate([vals, ones], axis=1)
            q = jnp.concatenate(
                [query[256 * m : 256 * m + 256, lo : lo + 128], query[512 + 64 * m : 576 + 64 * m, lo : lo + 128]], axis=0
            )
            score = dot_nt(q, keys) + mask_row[m]
            left, right = score[:, 0:128], score[:, 128:256]
            left = jnp.exp2(left - jnp.max(left, axis=-1, keepdims=True))
            right = jnp.exp2(right - jnp.max(right, axis=-1, keepdims=True))
            mixed = dot(jnp.concatenate([left, right], axis=1).astype(BF16), vals)
            mixed = (mixed[:, 0:128] / mixed[:, 128:256]).astype(BF16)
            att[256 * m : 256 * m + 256, lo : lo + 128] = mixed[0:256]
            att[512 + 64 * m : 576 + 64 * m, lo : lo + 128] = mixed[256:320]
    h3 = hid[...] + dot(att[...], bo_v[...])
    scale = lax.rsqrt(jnp.mean(h3 * h3, axis=-1, keepdims=True) + 1e-6)
    eps = dot_nt(head8[...].astype(BF16), (h3 * scale * b_gain[2:3, :]).astype(BF16))

    def step_of(noisy, eps, c0, c1, c2_, c3):
        c0, c1, c2_, c3 = (jnp.concatenate([c] * (eps.shape[1] // 128), axis=1) for c in (c0, c1, c2_, c3))
        clean = jnp.clip((noisy - c0 * eps) * c1, -1.0, 1.0)
        return clean, c2_ * clean + c3 * eps

    pick_k, pick_l = iota((256, 128), 0), iota((256, 128), 1)
    noisy = jnp.zeros((8, 128), F32)
    for m in range(2):
        whole = pltpu.roll(x8b[m], jnp.mod(0 - 256 * z, 1024), 1)[:, 0:256]
        _, prior = step_of(whole, eps[:, 256 * m : 256 * m + 256], *coefs(0, m))
        for c in range(3):
            early_v[0, c, m : m + 1, :] = prior[c : c + 1]
        spot = pick_l - 64 * m
        sel = (spot >= 0) & (spot < 64) & ((pick_k >> 5) == (spot >> 3)) & ((pick_k & 31) == (spot & 7))
        noisy += dot(x8b[m, :, 0:256].astype(BF16), sel.astype(F32).astype(BF16))
    first_half = iota((8, 128), 1) < 64
    mixed_coefs = tuple(jnp.where(first_half, a, b) for a, b in zip(coefs(0, 0), coefs(0, 1)))
    region, _ = step_of(noisy, eps[:, 512:640], *mixed_coefs)
    region = region.astype(BF16)

    def back(s, ms, h2, width):
        scale = lax.rsqrt(jnp.sum(h2 * h2, axis=0, keepdims=True) * (1.0 / 128.0) + 1e-6)
        q = (dot(wq_t[s], h2.astype(BF16)) * scale).astype(BF16)
        both = []
        for n, m in enumerate(ms):
            score = dot(kcat[2 * s + m], q[:, width * n : width * n + width])
            mask = jnp.concatenate([mask_col[m]] * (width // 128), axis=1)
            left, right = score[0:128] + mask, score[128:256] + mask
            left = jnp.exp2(left - jnp.max(left, axis=0, keepdims=True)).astype(BF16)
            right = jnp.exp2(right - jnp.max(right, axis=0, keepdims=True)).astype(BF16)
            mixed = dot(vcat[2 * s + m], jnp.concatenate([left, right], axis=0))
            top = mixed[0:64] * (1.0 / mixed[128:129])
            bottom = mixed[64:128] * (1.0 / mixed[129:130])
            both.append(jnp.concatenate([top, bottom], axis=0).astype(BF16))
        both = both[0] if len(both) == 1 else jnp.concatenate(both, axis=1)
        h3 = h2 + dot(wo_t[s], both)
        scale = lax.rsqrt(jnp.sum(h3 * h3, axis=0, keepdims=True) * (1.0 / 128.0) + 1e-6)
        return dot(wh_t[s], h3.astype(BF16)) * scale

    def activate(hidden, s, width):
        scale = lax.rsqrt(jnp.sum(hidden * hidden, axis=0, keepdims=True) * (1.0 / 128.0) + 1e-6)
        gain = jnp.concatenate([gcol[s]] * (width // 128), axis=1)
        half = hidden * scale * gain
        return half + half * jnp.tanh(half)

    lane1 = iota((1, 128), 1)

    def regroup(value, source, target):
        by = 32 * (target - source) % 128
        return pltpu.roll(value, by, 1) if by else value

    lanes = iota((1, 768), 1)
    lanes = jnp.where(lanes >= 384, lanes - 384, lanes)
    row_of = 8 * z - 2 + (lanes >> 5)
    col_of = lanes & 31
    inside = (row_of >= 0) & (row_of < 32)
    spread_k = iota((128, 384), 0)
    spread_l = iota((128, 384), 1)
    spread_at = (((8 * z + 2 + (spread_l >> 5)) >> 2) - 1) * 8 + ((spread_l & 31) >> 2)
    spread_at = jnp.where((spread_at >= 0) & (spread_at < 64), spread_at, -1000)
    which = iota((8, 384), 0)
    noisy, hidden = [], []
    for m in range(2):
        x = pltpu.roll(x8u[m], jnp.mod(64 - 256 * z, 1024), 1)[:, 0:384]
        cond = pltpu.roll(dot(region, (spread_k == spread_at + 64 * m).astype(F32).astype(BF16)), 3, 0)
        x8 = jnp.where(which < 3, x, jnp.where(which < 6, cond, 1.0))
        hidden.append(dot(gcol[2 + m, :, 0:8].astype(BF16), x8.astype(BF16)))
        noisy.append(x)
    hidden = jnp.concatenate(hidden, axis=1)
    active = jnp.where(inside, activate(hidden, 0, 768), 0.0)
    stack = [
        jnp.where(col_of == 0, 0.0, pltpu.roll(active, 1, 1)),
        active,
        jnp.where(col_of == 31, 0.0, pltpu.roll(active, 767, 1)),
    ]
    stack = [pltpu.roll(one, 32, 1) for one in stack] + stack + [pltpu.roll(one, 736, 1) for one in stack]
    stack = jnp.concatenate([one.astype(BF16) for one in stack], axis=0)
    eps = back(0, (0, 1), hidden + dot(conv_t[0], stack), 384)
    for m in range(2):
        clean, prior = step_of(noisy[m], eps[:, 384 * m : 384 * m + 384], *coefs(1, m))
        prior = pltpu.roll(prior, 320, 1)[:, 0:256]
        for c in range(3):
            early_v[1, c, m : m + 1, :] = prior[c : c + 1]
        clean = clean.astype(BF16).astype(F32)

        def rows_at(first):
            total = None
            for g in range(4):
                row = first + 2 * g
                one = regroup(clean[:, 128 * (row // 4) : 128 * (row // 4) + 128], row % 4, g)
                total = one if total is None else jnp.where((lane1 >> 5) == g, one, total)
            return total

        x2[m] = jnp.ones((34 * 8, 128), F32)
        even, odd = rows_at(2), rows_at(3)
        above, below = rows_at(1), rows_at(4)
        for c in range(3):
            x2[m, pl.ds(8 + 3 + c, 16, 8), :] = jnp.broadcast_to(even[c : c + 1], (16, 128))
            x2[m, pl.ds(8 * 17 + 3 + c, 16, 8), :] = jnp.broadcast_to(odd[c : c + 1], (16, 128))
            x2[m, 3 + c : 4 + c, :] = above[c : c + 1]
            x2[m, 33 * 8 + 3 + c : 33 * 8 + 4 + c, :] = below[c : c + 1]

    early_out = pltpu.make_async_copy(early_v, early, own_sems.at[2])
    early_out.start()
    each_other(z, y, k, lambda j: noise_to(j, j).wait_recv())

    @pl.when(z > 0)
    def _():
        noise_to(0, LANE).wait_recv()

    @pl.when(z < SEG - 1)
    def _():
        noise_to(0, LANE + 1).wait_recv()

    @pl.when(z == 0)
    def _():
        rcv[LANE] = jnp.zeros((32, 128), BF16)

    @pl.when(z == SEG - 1)
    def _():
        rcv[LANE + 1] = jnp.zeros((32, 128), BF16)

    blocks = [rcv[n].astype(F32)[0:24] for n in range(LANE + 2)]
    for m in range(2):
        edge = {}
        for h in range(2):
            for half in range(2):
                group = 2 * m + half
                total = regroup(blocks[h], group, 0)
                for g in range(1, 4):
                    total = jnp.where((lane1 >> 5) == g, regroup(blocks[2 * g + h], group, g), total)
                edge[h, half] = total
                for c in range(3):
                    x2[m, pl.ds(8 * (1 + 16 * h + 8 * half) + c, 8, 8), :] = total[8 * c : 8 * c + 8]
        top = regroup(blocks[LANE], 2 * m + 1, 0)
        low = regroup(blocks[LANE + 1], 2 * m, 3)
        over = pltpu.roll(edge[1, 1], 32, 1)
        under = pltpu.roll(edge[0, 0], 96, 1)
        for c in range(3):
            x2[m, c : c + 1, :] = jnp.where(lane1 < 32, top, over)[8 * c + 7 : 8 * c + 8]
            x2[m, 33 * 8 + c : 33 * 8 + c + 1, :] = jnp.where(lane1 >= 96, low, under)[8 * c : 8 * c + 1]

    def result_to(m, j, slot):
        return remote(snd2.at[m, j], rcv2.at[m, slot], send2.at[m, j], recv2.at[m, slot], y, z * LANE + j)

    def own_to(m):
        return pltpu.make_async_copy(snd2.at[m, k], rcv2.at[m, k], own_sems.at[m])

    FT = 17
    lanef = iota((1, 128 * FT), 1)
    colf = iota((1, 128), 1) & 31
    for m in range(2):
        for n in range(34 // FT):
            t = n * FT
            rows = x2[m, t * 8 : (t + FT) * 8, :]
            x8 = jnp.concatenate([rows[8 * e : 8 * e + 8] for e in range(FT)], axis=1).astype(BF16)
            hidden = dot(gcol[4 + m, :, 0:8].astype(BF16), x8)
            active = activate(hidden, 1, 128 * FT)
            if n == 0:
                active = jnp.where((lanef < 32) & (z == 0), 0.0, active)
            else:
                active = jnp.where((lanef >= 128 * FT - 32) & (z == SEG - 1), 0.0, active)
            for h in range(FT):
                one = active[:, 128 * h : 128 * h + 128]
                hid3[m, t + h] = hidden[:, 128 * h : 128 * h + 128]
                act3[m, t + h, 0:128] = jnp.where(colf == 0, 0.0, pltpu.roll(one, 1, 1)).astype(BF16)
                act3[m, t + h, 128:256] = one.astype(BF16)
                act3[m, t + h, 256:384] = jnp.where(colf == 31, 0.0, pltpu.roll(one, 127, 1)).astype(BF16)

        for i in range(0, 32, STEPS):
            tiles = [act3[m, i + e] for e in range(STEPS + 2)]
            stack = jnp.concatenate(
                [jnp.concatenate(tiles[a : a + STEPS], axis=1) for a in range(3)], axis=0
            )
            h2 = jnp.concatenate([hid3[m, i + 1 + e] for e in range(STEPS)], axis=1) + dot(conv_t[1], stack)
            eps = back(1, (m,), h2, 128 * STEPS)
            rows = x2[m, (i + 1) * 8 : (i + 1 + STEPS) * 8, :]
            noisy = jnp.concatenate([rows[8 * e : 8 * e + 8] for e in range(STEPS)], axis=1)
            clean, prior = step_of(noisy, eps, *coefs(2, m))
            for e in range(STEPS):
                c2[0, m, (i + e) * 8 : (i + e) * 8 + 8, :] = clean[:, 128 * e : 128 * e + 128]
                c2[1, m, (i + e) * 8 : (i + e) * 8 + 8, :] = prior[:, 128 * e : 128 * e + 128]

        for j in range(LANE):
            rows = []
            for c in range(3):
                total = None
                for o in range(2):
                    for half in range(2):
                        one = c2[o, m, pl.ds(128 * (j % 2) + 64 * half + c, 8, 8), :]
                        one = regroup(one, j // 2, 2 * o + half)
                        total = one if total is None else jnp.where((lane1 >> 5) == 2 * o + half, one, total)
                rows.append(total)
            rows.append(jnp.zeros((8, 128), F32))
            snd2[m, j] = jnp.concatenate(rows, axis=0).astype(BF16)

        each_other(z, y, k, lambda j: result_to(m, j, k).start())

        @pl.when(y == z)
        def _():
            own_to(m).start()

    each_other(z, y, k, lambda j: noise_to(j, k).wait_send())
    for cond, slot, step in ((lower, LANE, 1), (upper, LANE + 1, -1)):
        @pl.when(cond)
        def _():
            for j in range(LANE):
                halo_to(j, slot, y + step).wait_send()

    for m in range(2):
        each_other(z, y, k, lambda j: result_to(m, j, j).wait_recv())
    for m in range(2):
        each_other(z, y, k, lambda j: result_to(m, j, k).wait_send())

    @pl.when(y == z)
    def _():
        for m in range(2):
            own_to(m).wait()

    early_out.wait()


def unpack_kernel(early_in, got, early, out):
    early[...] = early_in[...].astype(BF16)
    for m in range(1):
        for j in range(LANE):
            whole = got[m, j].astype(F32)[0:24]
            for o in range(2):
                upper, lower = (
                    pltpu.roll(whole, (128 - 32 * (2 * o + half)) % 128, 1)[:, 0:32] if 2 * o + half else whole[:, 0:32]
                    for half in range(2)
                )
                for c in range(3):
                    both = jnp.concatenate([upper[8 * c : 8 * c + 8], lower[8 * c : 8 * c + 8]], axis=0)
                    out[o, m, j, c] = both.astype(BF16)


def shards(
    text_states, token_ids, step_ids, base_noise, upscale_noise, final_noise, t5_gain,
    base_keyval, upscale_keyval, base_input, base_time, base_gain, base_conv, base_query,
    base_output, base_head, upscale_input, upscale_time, upscale_gain, upscale_conv,
    upscale_query, upscale_output, upscale_head,
):
    early, got = pl.pallas_call(
        step_kernel,
        out_shape=(
            jax.ShapeDtypeStruct((2, 3, 2, 256), F32),
            jax.ShapeDtypeStruct((2, LANE, 32, 128), BF16),
        ),
        in_specs=[SMEM] + [VMEM] * 10 + [ANY] * 12,
        out_specs=(ANY, ANY),
        scratch_shapes=[
            pltpu.VMEM((256, 4096), BF16),
            pltpu.VMEM((3, 4096, 512), BF16),
            pltpu.VMEM((512, 512), BF16),
            pltpu.VMEM((4608, 512), BF16),
            pltpu.VMEM((512, 512), BF16),
            pltpu.VMEM((512, 512), BF16),
            pltpu.VMEM((2, 128, 128), BF16),
            pltpu.VMEM((2, 9, 128, 128), BF16),
            pltpu.VMEM((2, 128, 128), BF16),
            pltpu.VMEM((2, 128, 128), BF16),
            pltpu.VMEM((2, LANE, 3, 16, 32), BF16),
            pltpu.VMEM((256, 4096), BF16),
            pltpu.VMEM((256, 1536), BF16),
            pltpu.VMEM((640, 4608), BF16),
            pltpu.VMEM((640, 512), F32),
            pltpu.VMEM((640, 512), BF16),
            pltpu.VMEM((640, 512), BF16),
            pltpu.VMEM((2, 8, 1024), F32),
            pltpu.VMEM((2, 8, 1024), F32),
            pltpu.VMEM((8, 128), F32),
            pltpu.VMEM((8, 128), F32),
            pltpu.VMEM((6, 128, 128), F32),
            pltpu.VMEM((2, 128, 128), BF16),
            pltpu.VMEM((2, 128, 128), BF16),
            pltpu.VMEM((2, 8, 128), BF16),
            pltpu.VMEM((2, 128, 1152), BF16),
            pltpu.VMEM((4, 256, 128), BF16),
            pltpu.VMEM((4, 144, 256), BF16),
            pltpu.VMEM((2, 1, 256), F32),
            pltpu.VMEM((2, 128, 128), F32),
            pltpu.VMEM((8, 512), F32),
            pltpu.VMEM((2, 272, 128), F32),
            pltpu.VMEM((2, 34, 128, 128), F32),
            pltpu.VMEM((2, 34, 384, 128), BF16),
            pltpu.VMEM((2, 2, 256, 128), F32),
            pltpu.VMEM((2, 3, 2, 256), F32),
            pltpu.VMEM((LANE, 32, 128), F32),
            pltpu.VMEM((LANE, 32, 128), BF16),
            pltpu.VMEM((LANE + 2, 32, 128), BF16),
            pltpu.VMEM((2, LANE, 32, 128), BF16),
            pltpu.SemaphoreType.DMA((16,)),
            pltpu.SemaphoreType.DMA((LANE,)),
            pltpu.SemaphoreType.DMA((LANE + 2,)),
            pltpu.SemaphoreType.DMA((LANE,)),
            pltpu.SemaphoreType.DMA((2, LANE)),
            pltpu.SemaphoreType.DMA((2, LANE)),
            pltpu.SemaphoreType.DMA((3,)),
        ],
        compiler_params=pltpu.CompilerParams(
            vmem_limit_bytes=56 * 1024 * 1024, collective_id=0, has_side_effects=True
        ),
        name="denoise",
    )(
        step_ids.T, token_ids, base_noise[:, 0].transpose(1, 0, 2), upscale_noise[:, 0].transpose(1, 0, 2), t5_gain[None],
        base_input, base_gain, base_head.T, upscale_input.transpose(1, 0, 2), upscale_gain.transpose(1, 0, 2),
        upscale_head.transpose(2, 0, 1), final_noise,
        text_states.reshape(256, 4096), base_keyval, upscale_keyval, base_time, base_conv.reshape(4608, 512),
        base_query, base_output, upscale_time, upscale_conv, upscale_query, upscale_output,
    )
    early, final_states = pl.pallas_call(
        unpack_kernel,
        out_shape=(
            jax.ShapeDtypeStruct((2, 3, 2, 256), BF16),
            jax.ShapeDtypeStruct((2, 2, LANE, 3, 16, 32), BF16),
        ),
        grid=(2,),
        in_specs=[
            pl.BlockSpec((2, 3, 2, 256), lambda m: (0, 0, 0, 0)),
            pl.BlockSpec((1, LANE, 32, 128), lambda m: (m, 0, 0, 0)),
        ],
        out_specs=(
            pl.BlockSpec((2, 3, 2, 256), lambda m: (0, 0, 0, 0)),
            pl.BlockSpec((2, 1, LANE, 3, 16, 32), lambda m: (0, m, 0, 0, 0, 0)),
        ),
        compiler_params=pltpu.CompilerParams(vmem_limit_bytes=60 * 1024 * 1024),
        name="unpack",
    )(early, got)
    return early.transpose(0, 2, 1, 3)[:, :, None], final_states


def solution(mesh):
    placed = [P() for _ in range(23)]
    placed[0] = placed[3] = placed[4] = P(None, "space", None, None)
    placed[5] = P(None, None, None, "space", None)
    return jax.shard_map(
        shards,
        mesh=mesh,
        in_specs=tuple(placed),
        out_specs=(
            P(None, None, "space", None, "segment"),
            P(None, None, "segment", None, "space", None),
        ),
        check_vma=False,
    )
```
